512 devices in a mesh: seq: 128 (over y, z, core), head: 4 (over x).
Axes of the slice: x: 4, y: 8, z: 8, core: 2. Of those that a mesh axis runs over, the one named last changes fastest.
Arguments:
- queries: bfloat16 [32768, 1024], P('seq', 'head'), may hold values from -8 to 8
- key_rows: bfloat16 [32768, 1024], P('seq', 'head'), may hold values from -8 to 8
- value_rows: bfloat16 [32768, 1024], P('seq', 'head'), may hold values from -6 to 6
- attn_out_grad: bfloat16 [32768, 1024], P('seq', 'head'), may hold values from -6 to 6
- ssm_input: bfloat16 [32768, 512], P('seq', 'head'), may hold values from -6 to 6
- b_matrix: bfloat16 [32768, 256], P('seq'), may hold values from -2 to 2
- c_matrix: bfloat16 [32768, 256], P('seq'), may hold values from -2 to 2
- step_sizes: float32 [32768, 8], P('seq', 'head'), may hold values from 0.005 to 0.05
- decay_rates: float32 [8], P('head'), may hold values from 1.5258789e-05 to 0.5
- skip_gain: float32 [8], P('head'), may hold values from 0.5 to 1.5
- ssm_out_grad: bfloat16 [32768, 512], P('seq', 'head'), may hold values from -6 to 6
- doc_lengths: int32 [128], replicated, may hold values from 1 to 512, 32768 in all
Outputs:
- attn_out: bfloat16 [32768, 1024], P('seq', 'head')
- query_grad: bfloat16 [32768, 1024], P('seq', 'head')
- key_grad: bfloat16 [32768, 1024], P('seq', 'head')
- value_grad: bfloat16 [32768, 1024], P('seq', 'head')
- ssm_out: bfloat16 [32768, 512], P('seq', 'head')
- input_grad: bfloat16 [32768, 512], P('seq', 'head')
- b_grad: float32 [32768, 256], P('seq')
- c_grad: float32 [32768, 256], P('seq')
The draws below stay inside these ranges and needn't reach their ends.
All inputs are finite; a program needn't handle non-finite values.
Results may differ from the reference program's by a relative error of at most 0.022.
Values may be sent and summed in bfloat16 or wider, within the bound.
A program may use at most 128 MiB of HBM per device.

```python
import math
import jax
import jax.numpy as jnp
import numpy as np
from jax import lax

HEAD_DIM = 128
SSM_DIM = 64
STATE = 256
TOK_DEV = 256
MOST_DOC = 512
ATT_HEADS = 8
SSM_HEADS = 8
REACH = 2
SEQ_LEN = 32768
DOCS = 128
N_SEQ = 128


def paired_rows(key):
    paired_key = jax.random.fold_in(key, 4111)
    draw_one, draw_two = jax.random.split(paired_key, 2)
    array_shape = (SEQ_LEN, ATT_HEADS * HEAD_DIM)
    query_part = jax.random.normal(draw_one, array_shape, jnp.float32)
    key_part = jax.random.normal(draw_two, array_shape, jnp.float32)
    return (jnp.clip(query_part, -8.0, 8.0), jnp.clip(key_part, -8.0, 8.0))


def draw_queries(key, part):
    return paired_rows(key)[0].astype(jnp.bfloat16)


def draw_key_rows(key, part):
    return paired_rows(key)[1].astype(jnp.bfloat16)


def level_of(key, shape, cuts, smallest, high):
    loudness, own = 1.0, jax.random.fold_in(key, 6)
    for axis_at, blocks in cuts:
        steps = jnp.exp(jax.random.uniform(jax.random.fold_in(own, axis_at), (blocks,), jnp.float32, smallest / len(cuts), high / len(cuts)))
        loudness = loudness * jnp.repeat(steps, shape[axis_at] // blocks).reshape([-1 if axis == axis_at else 1 for axis in range(len(shape))])
    return loudness


def profile(count, total, reach, slope):
    portions = [(1 << 20) // math.isqrt(grade ** slope) + 1 for grade in range(2, count + 1)]
    surplus, given = total - reach - (count - 1), [1] * (count - 1)
    while surplus > 0:
        free = [i for i in range(count - 1) if given[i] < reach]
        mass, left = sum([portions[i] for i in free]), surplus
        for i in free:
            more = min(reach - given[i], max(1, left * portions[i] // mass), surplus)
            given[i] = given[i] + more
            surplus = surplus - more
    return np.array([reach] + given)


def ragged(stream_key, number_of, total, most, lean):
    if number_of == 2:
        one = jax.random.randint(stream_key, (), max(1, total - most), min(most, total - 1) + 1)
        return jnp.stack([one, total - one])
    tallies = jnp.asarray(profile(number_of, total, most, lean), jnp.int32)
    twos = (number_of - 1) // 2
    source_of, taker = tallies[1:1 + 2 * twos:2], tallies[2:2 + 2 * twos:2]
    margin = jnp.minimum(source_of - 1, most - taker)
    shifted = jax.random.randint(jax.random.fold_in(stream_key, 1), (twos,), 0, 1 << 20) % (margin + 1)
    tallies = tallies.at[1:1 + 2 * twos:2].set(source_of - shifted).at[2:2 + 2 * twos:2].set(taker + shifted)
    return tallies[jax.random.permutation(jax.random.fold_in(stream_key, 2), number_of)]


def normal_values(own_key, shape, spread, bound, pieces=(), kind=jnp.bfloat16):
    result = jax.random.normal(own_key, shape, jnp.float32) * spread
    if len(pieces) > 0:
        result = level_of(own_key, shape, pieces, -0.22, 0.18) * result
    return jnp.clip(result, min=-bound, max=bound).astype(kind)


def setup_inputs(seed: int = 0) -> dict:
    streams_of = jax.random.split(jax.random.key(seed), 13)
    queries = draw_queries(jax.random.fold_in(streams_of[12], 71), 0)
    key_rows = draw_key_rows(jax.random.fold_in(streams_of[12], 71), 0)
    value_rows = normal_values(streams_of[2], (SEQ_LEN, ATT_HEADS * HEAD_DIM), 1.0, 6.0, ((0, 128), (1, 4)))
    attn_out_grad = normal_values(streams_of[3], (SEQ_LEN, ATT_HEADS * HEAD_DIM), 1.0, 6.0, ((0, 128), (1, 4)))
    ssm_input = normal_values(streams_of[4], (SEQ_LEN, SSM_HEADS * SSM_DIM), 1.0, 6.0, ((0, 128), (1, 4)))
    b_matrix = normal_values(streams_of[5], (SEQ_LEN, STATE), 0.25, 2.0, ((0, 128),))
    c_matrix = normal_values(streams_of[6], (SEQ_LEN, STATE), 0.25, 2.0, ((0, 128),))
    step_sizes = jnp.clip(jnp.exp(math.log(0.05) - 2.3025851 * jax.random.uniform(streams_of[7], (SEQ_LEN, SSM_HEADS), jnp.float32) ** level_of(streams_of[7], (SEQ_LEN, SSM_HEADS), ((0, 128), (1, 4)), -0.2, 0.2)), 0.005, 0.05)
    decay_rates = jnp.clip(jnp.exp(math.log(0.5) - 10.3972077 * jax.random.uniform(streams_of[8], (SSM_HEADS,), jnp.float32) ** level_of(streams_of[8], (SSM_HEADS,), ((0, 4),), -0.2, 0.2)), 1.52587890625e-05, 0.5)
    skip_gain = jnp.clip(1.0 + 0.1 * jax.random.normal(streams_of[9], (SSM_HEADS,), jnp.float32), 0.5, 1.5)
    ssm_out_grad = normal_values(streams_of[10], (SEQ_LEN, SSM_HEADS * SSM_DIM), 1.0, 6.0, ((0, 128), (1, 4)))
    doc_lengths = ragged(streams_of[11], DOCS, SEQ_LEN, MOST_DOC, 2).astype(jnp.int32)
    return {"queries": queries, "key_rows": key_rows, "value_rows": value_rows, "attn_out_grad": attn_out_grad, "ssm_input": ssm_input, "b_matrix": b_matrix, "c_matrix": c_matrix, "step_sizes": step_sizes, "decay_rates": decay_rates, "skip_gain": skip_gain, "ssm_out_grad": ssm_out_grad, "doc_lengths": doc_lengths}


def doc_index(positions, doc_ends):
    return lax.optimization_barrier(jnp.sum((positions[:, None] >= doc_ends[None, :]).astype(jnp.int32), axis=1))

def visible_mask(query_pos, key_pos, doc_ends):
    same_doc = doc_index(query_pos, doc_ends)[:, None] == doc_index(key_pos, doc_ends)[None, :]
    return same_doc & (key_pos[None, :] <= query_pos[:, None]) & (key_pos[None, :] >= 0)

def attention(queries, key_rows, value_rows, attn_out_grad, doc_ends):
    columns = queries.shape[1]
    head_count = columns // HEAD_DIM
    window_rows = (REACH + 1) * TOK_DEV
    scale = HEAD_DIM ** (-0.5)
    front_pad = jnp.zeros((REACH * TOK_DEV, columns), queries.dtype)
    key_pad = jnp.concatenate([front_pad, key_rows], axis=0)
    value_pad = jnp.concatenate([front_pad, value_rows], axis=0)
    acc_pad = jnp.zeros(((N_SEQ + REACH) * TOK_DEV, columns), jnp.float32)

    def scan_step(running, block_index):
        key_acc, value_acc = running
        row_start = (block_index * TOK_DEV).astype(jnp.int32)
        query_block = lax.dynamic_slice_in_dim(queries, row_start, TOK_DEV, 0).reshape(TOK_DEV, head_count, HEAD_DIM).astype(jnp.float32)
        grad_block = lax.dynamic_slice_in_dim(attn_out_grad, row_start, TOK_DEV, 0).reshape(TOK_DEV, head_count, HEAD_DIM).astype(jnp.float32)
        key_block = lax.dynamic_slice_in_dim(key_pad, row_start, window_rows, 0).reshape(window_rows, head_count, HEAD_DIM).astype(jnp.float32)
        value_block = lax.dynamic_slice_in_dim(value_pad, row_start, window_rows, 0).reshape(window_rows, head_count, HEAD_DIM).astype(jnp.float32)
        query_pos = row_start + jnp.arange(TOK_DEV, dtype=jnp.int32)
        key_pos = row_start - REACH * TOK_DEV + jnp.arange(window_rows, dtype=jnp.int32)
        tile_mask = visible_mask(query_pos, key_pos, doc_ends)[None]
        scores = jnp.einsum('thd,shd->hts', query_block, key_block) * scale
        scores = jnp.where(tile_mask, scores, -jnp.inf)
        row_top = lax.optimization_barrier(jnp.max(scores, axis=-1, keepdims=True))
        row_total = lax.optimization_barrier(jnp.sum(jnp.exp(scores - row_top), axis=-1, keepdims=True))
        tile_probs = jnp.where(tile_mask, jnp.exp(scores - row_top) / row_total, 0.0)
        probs_low = lax.optimization_barrier(tile_probs.astype(jnp.bfloat16)).astype(jnp.float32)
        attn_block = jnp.einsum('hts,shd->thd', probs_low, value_block).astype(jnp.bfloat16)
        row_delta = jnp.einsum('thd,thd->ht', grad_block, attn_block.astype(jnp.float32))
        prob_grad = jnp.einsum('thd,shd->hts', grad_block, value_block)
        dscore = (tile_probs * (prob_grad - row_delta[:, :, None]) * scale).astype(jnp.bfloat16)
        dscore = lax.optimization_barrier(dscore).astype(jnp.float32)
        query_part = jnp.einsum('hts,shd->thd', dscore, key_block).astype(jnp.bfloat16)
        key_part = jnp.einsum('hts,thd->shd', dscore, query_block).reshape(window_rows, columns)
        value_part = jnp.einsum('hts,thd->shd', probs_low, grad_block).reshape(window_rows, columns)
        key_acc = lax.dynamic_update_slice_in_dim(key_acc, lax.dynamic_slice_in_dim(key_acc, row_start, window_rows, 0) + key_part, row_start, 0)
        value_acc = lax.dynamic_update_slice_in_dim(value_acc, lax.dynamic_slice_in_dim(value_acc, row_start, window_rows, 0) + value_part, row_start, 0)
        return ((key_acc, value_acc), (attn_block.reshape(TOK_DEV, columns), query_part.reshape(TOK_DEV, columns)))
    (key_acc, value_acc), (attn_blocks, query_blocks) = lax.scan(scan_step, (acc_pad, acc_pad), jnp.arange(N_SEQ, dtype=jnp.int32))
    attn_out = attn_blocks.reshape(N_SEQ * TOK_DEV, columns)
    query_grad = query_blocks.reshape(N_SEQ * TOK_DEV, columns)
    key_grad = key_acc[REACH * TOK_DEV:].astype(jnp.bfloat16)
    value_grad = value_acc[REACH * TOK_DEV:].astype(jnp.bfloat16)
    return (attn_out, query_grad, key_grad, value_grad)

def ssm_parts(x_heads, b_rows, c_rows, step_sizes, decay_rates, skip_gain):
    row_count = x_heads.shape[0]
    offsets = jnp.arange(row_count, dtype=jnp.int32)
    log_decay = jnp.cumsum(-step_sizes * decay_rates[None, :], axis=0)
    causal = offsets[None, :] <= offsets[:, None]
    log_gaps = log_decay.T[:, :, None] - log_decay.T[:, None, :]
    fading = jnp.where(causal[None], jnp.exp(jnp.where(causal[None], log_gaps, 0.0)), 0.0)
    intersection = jnp.dot(c_rows, b_rows.T, precision=lax.Precision.HIGHEST)
    mixing = intersection[None] * fading * step_sizes.T[:, None, :]
    direct = jnp.einsum('hts,shp->thp', mixing, x_heads, precision=lax.Precision.HIGHEST)
    direct = direct + skip_gain[None, :, None] * x_heads
    carry_weight = jnp.exp(log_decay)
    tail_weight = jnp.exp(log_decay[-1][None, :] - log_decay) * step_sizes
    local_state = jnp.einsum('th,tn,thp->hnp', tail_weight, b_rows, x_heads, precision=lax.Precision.HIGHEST)
    decay_all = jnp.exp(log_decay[-1])
    return (direct, local_state, decay_all, carry_weight)

def ssm_forward(x_all, b_all, c_all, step_sizes, decay_rates, skip_gain):
    head_count = decay_rates.shape[0]
    x_blocks = x_all.reshape(N_SEQ, TOK_DEV, head_count, -1)
    b_blocks = b_all.reshape(N_SEQ, TOK_DEV, -1)
    c_blocks = c_all.reshape(N_SEQ, TOK_DEV, -1)
    step_blocks = step_sizes.reshape(N_SEQ, TOK_DEV, head_count)

    def scan_step(carry_state, block_items):
        x_heads, b_rows, c_rows, step_block = block_items
        direct, local_state, decay_all, carry_weight = ssm_parts(x_heads, b_rows, c_rows, step_block, decay_rates, skip_gain)
        incoming = jnp.einsum('tn,hnp->thp', c_rows, carry_state, precision=lax.Precision.HIGHEST)
        ssm_rows = direct + carry_weight[:, :, None] * incoming
        return (decay_all[:, None, None] * carry_state + local_state, ssm_rows)
    state_zero = jnp.zeros((head_count, b_all.shape[1], x_blocks.shape[-1]), x_all.dtype)
    items = (x_blocks, b_blocks, c_blocks, step_blocks)
    _, ssm_blocks = lax.scan(jax.checkpoint(scan_step), state_zero, items)
    return ssm_blocks.reshape(x_all.shape)

def reference(queries, key_rows, value_rows, attn_out_grad, ssm_input, b_matrix, c_matrix, step_sizes, decay_rates, skip_gain, ssm_out_grad, doc_lengths):
    doc_ends = jnp.cumsum(doc_lengths, dtype=jnp.int32)
    attn_out, query_grad, key_grad, value_grad = attention(queries, key_rows, value_rows, attn_out_grad, doc_ends)

    def forward(x_value, b_value, c_value):
        return ssm_forward(x_value, b_value, c_value, step_sizes, decay_rates, skip_gain)
    ssm_rows, pullback = jax.vjp(forward, ssm_input.astype(jnp.float32), b_matrix.astype(jnp.float32), c_matrix.astype(jnp.float32))
    x_grad, b_grad, c_grad = pullback(ssm_out_grad.astype(jnp.float32))
    return (attn_out, query_grad, key_grad, value_grad, ssm_rows.astype(jnp.bfloat16), x_grad.astype(jnp.bfloat16), b_grad, c_grad)
```

```python
import functools

import jax
import jax.numpy as jnp
from jax import lax
from jax.experimental import pallas as pl
from jax.experimental.pallas import tpu as pltpu
from jax.sharding import PartitionSpec as P

MESH = pl.DeviceIdType.MESH
HEAD_DIM = 128
SCALE = HEAD_DIM**-0.5
OFF = -1e30
F32 = jnp.float32
BF16 = jnp.bfloat16
VMEM_BYTES = 40 * 1024 * 1024


def dot(a, b):
    return jnp.dot(a, b, preferred_element_type=F32)


def dot_nt(a, b):
    return lax.dot_general(a, b, (((1,), (1,)), ((), ())), preferred_element_type=F32)


def dot_tn(a, b):
    return lax.dot_general(a, b, (((0,), (0,)), ((), ())), preferred_element_type=F32)


def iota(shape, axis):
    return lax.broadcasted_iota(jnp.int32, shape, axis)


def lower(size):
    return iota((size, size), 1) <= iota((size, size), 0)


def doc_start_column(doc_ref, first, rows):
    docs = doc_ref.shape[1]
    lengths = jnp.broadcast_to(doc_ref[...], (16, docs))
    upper = jnp.where(iota((docs, docs), 0) <= iota((docs, docs), 1), 1.0, 0.0).astype(BF16)
    high, low = lengths // 16, lengths % 16
    ends = 16.0 * dot(high.astype(F32).astype(BF16), upper) + dot(
        low.astype(F32).astype(BF16), upper
    )
    ends = jnp.broadcast_to(ends[0:1, :], (rows, docs))
    position = (first + iota((rows, docs), 0)).astype(F32)
    return jnp.max(jnp.where(ends <= position, ends, 0.0), axis=1, keepdims=True)


def running_sum(rows):
    ones = jnp.where(lower(rows.shape[0]), 1.0, 0.0).astype(BF16)
    high = rows.astype(BF16)
    rest = rows - high.astype(F32)
    middle = rest.astype(BF16)
    low = (rest - middle.astype(F32)).astype(BF16)
    return dot(ones, high) + dot(ones, middle) + dot(ones, low)


def main_kernel(
    n_seq,
    n_head,
    n_z,
    rate_ref,
    gain_ref,
    doc_ref,
    q_ref,
    k_ref,
    v_ref,
    do_ref,
    x_ref,
    g_ref,
    b_ref,
    c_ref,
    dt_ref,
    attn_ref,
    dq_ref,
    dk_ref,
    dv_ref,
    y_ref,
    xg_ref,
    mix_ref,
    state_ref,
    kv_in,
    qd_in,
    stat_out,
    stat_in,
    a_src,
    a_dst,
    la_src,
    la_dst,
    scan_buf,
    cum_buf,
    t_src,
    t_dst,
    tl_src,
    tl_dst,
    r_src,
    r_dst,
    near_send,
    near_recv,
    stat_send,
    stat_recv,
    a_send,
    a_recv,
    la_send,
    la_recv,
    t_send,
    t_recv,
    tl_send,
    tl_recv,
    r_send,
    r_recv,
    mix_send,
    mix_recv,
    state_send,
    state_recv,
):
    me = lax.axis_index("seq")
    hx = lax.axis_index("head")
    row = 2 * n_z
    n_y = n_seq // row
    rows = q_ref.shape[0]
    group, pos = me // row, me % row
    core = pos % 2
    base = group * row
    width = rows // n_z

    def seq_at(offset):
        return (me + offset + n_seq) % n_seq

    def slot_of(index, count, side):
        return index + side * (count - 1 - 2 * index)

    barrier = pltpu.get_barrier_semaphore()

    def greet(seq_index, head_index):
        pl.semaphore_signal(
            barrier, inc=1, device_id=(seq_index, head_index), device_id_type=MESH
        )

    for offset in (-2, -1, 1, 2):
        greet(seq_at(offset), hx)

    def greet_row(k, carry):
        greet(base + (pos + k) % row, hx)
        return carry

    lax.fori_loop(1, row, greet_row, 0)

    def greet_group(k, carry):
        greet(((group + k) % n_y) * row + pos, hx)
        return carry

    lax.fori_loop(1, n_y, greet_group, 0)
    for k in range(1, n_head):
        greet(me, (hx + k) % n_head)

    lanes_low = iota((rows, 128), 1) < 64
    dt_wide = jnp.concatenate(
        [
            jnp.broadcast_to(dt_ref[0:1, :], (64, rows)),
            jnp.broadcast_to(dt_ref[1:2, :], (64, rows)),
        ],
        axis=0,
    ).T
    rate_wide = jnp.where(lanes_low, rate_ref[0], rate_ref[1])
    gain_wide = jnp.where(lanes_low, gain_ref[0], gain_ref[1])
    log_decay = running_sum(-dt_wide * rate_wide)
    carry_weight = jnp.exp(log_decay)
    source_weight = jnp.exp(-log_decay) * dt_wide
    last = log_decay[rows - 1 : rows, :]
    decay_all = jnp.exp(last)
    mix_ref[hx, 0] = (carry_weight * g_ref[...].astype(F32)).astype(BF16)
    mix_ref[hx, 1] = (source_weight * x_ref[...].astype(F32)).astype(BF16)
    local_state = (decay_all * dot_tn(b_ref[...], mix_ref[hx, 1])).astype(BF16)
    local_adjoint = dot_tn(c_ref[...], mix_ref[hx, 0]).astype(BF16)
    for z in range(n_z):
        a_src[2 * z] = local_state[z * width : (z + 1) * width, :]
        a_src[2 * z + 1] = local_adjoint[z * width : (z + 1) * width, :]
    la_src[...] = last

    pl.semaphore_wait(barrier, 4 + (row - 1) + (n_y - 1) + (n_head - 1))

    def a_copies(k):
        owner = (pos + k) % row
        slot = slot_of(pos, row, owner % 2)
        target = (base + owner, hx)
        return (
            pltpu.make_async_remote_copy(
                a_src.at[owner], a_dst.at[slot], a_send.at[k], a_recv.at[slot], target, MESH
            ),
            pltpu.make_async_remote_copy(
                la_src, la_dst.at[slot], la_send.at[k], la_recv.at[slot], target, MESH
            ),
        )

    def a_start(k, carry):
        for copy in a_copies(k):
            copy.start()
        return carry

    lax.fori_loop(1, row, a_start, 0)
    own_slot = slot_of(pos, row, core)
    a_dst[own_slot] = a_src[pos]
    la_dst[own_slot] = la_src[...]

    near = []
    for distance in (1, 2):
        for part, (fore, back) in enumerate(((k_ref, q_ref), (v_ref, do_ref))):
            at = (distance - 1) * 2 + part
            near.append(
                pltpu.make_async_remote_copy(
                    fore,
                    kv_in.at[distance - 1, part],
                    near_send.at[at],
                    near_recv.at[at],
                    (seq_at(distance), hx),
                    MESH,
                )
            )
            near.append(
                pltpu.make_async_remote_copy(
                    back,
                    qd_in.at[distance - 1, part],
                    near_send.at[4 + at],
                    near_recv.at[4 + at],
                    (seq_at(-distance), hx),
                    MESH,
                )
            )
    for copy in near:
        copy.start()

    def over_head(ref, send, recv):
        return [
            pltpu.make_async_remote_copy(
                ref.at[hx],
                ref.at[hx],
                send.at[k],
                recv.at[hx],
                (me, (hx + k) % n_head),
                MESH,
            )
            for k in range(1, n_head)
        ]

    def from_head(ref, send, recv):
        for k in range(1, n_head):
            other = (hx + k) % n_head
            pltpu.make_async_remote_copy(
                ref.at[hx], ref.at[other], send.at[k], recv.at[other], (me, other), MESH
            ).wait_recv()

    mix_copies = over_head(mix_ref, mix_send, mix_recv)
    for copy in mix_copies:
        copy.start()

    causal = lower(rows)
    meet = jnp.where(causal, dot_nt(c_ref[...], b_ref[...]), 0.0).astype(BF16)
    y_inner = dot(meet, mix_ref[hx, 1])
    meet_back = jnp.where(
        iota((rows, rows), 0) <= iota((rows, rows), 1), dot_nt(b_ref[...], c_ref[...]), 0.0
    ).astype(BF16)
    x_inner = dot(meet_back, mix_ref[hx, 0])

    def a_wait(k, carry):
        slot = (own_slot + k) % row
        pltpu.make_async_remote_copy(
            a_src.at[0], a_dst.at[slot], a_send.at[k], a_recv.at[slot], (me, hx), MESH
        ).wait_recv()
        pltpu.make_async_remote_copy(
            la_src, la_dst.at[slot], la_send.at[k], la_recv.at[slot], (me, hx), MESH
        ).wait_recv()
        return carry

    lax.fori_loop(1, row, a_wait, 0)

    state = jnp.zeros((width, 128), F32)
    summed = jnp.zeros((1, 128), F32)
    for slot in range(row):
        scan_buf[slot] = state
        cum_buf[slot] = summed
        state = jnp.exp(la_dst[slot]) * state + a_dst[slot].astype(F32)
        summed = summed + la_dst[slot]
    t_src[...] = state.astype(BF16)
    tl_src[...] = summed

    own_group = slot_of(group, n_y, core)

    def t_copies(k):
        target = (((group + k) % n_y) * row + pos, hx)
        return (
            pltpu.make_async_remote_copy(
                t_src, t_dst.at[own_group], t_send.at[k], t_recv.at[own_group], target, MESH
            ),
            pltpu.make_async_remote_copy(
                tl_src, tl_dst.at[own_group], tl_send.at[k], tl_recv.at[own_group], target, MESH
            ),
        )

    def t_start(k, carry):
        for copy in t_copies(k):
            copy.start()
        return carry

    lax.fori_loop(1, n_y, t_start, 0)
    t_dst[own_group] = t_src[...]
    tl_dst[own_group] = tl_src[...]

    first = me * rows
    start_column = doc_start_column(doc_ref, first, rows)

    def t_wait(k, carry):
        slot = (own_group + k) % n_y
        pltpu.make_async_remote_copy(
            t_src, t_dst.at[slot], t_send.at[k], t_recv.at[slot], (me, hx), MESH
        ).wait_recv()
        pltpu.make_async_remote_copy(
            tl_src, tl_dst.at[slot], tl_send.at[k], tl_recv.at[slot], (me, hx), MESH
        ).wait_recv()
        return carry

    lax.fori_loop(1, n_y, t_wait, 0)
    carried = jnp.zeros((width, 128), F32)
    for slot in range(n_y):
        grown = jnp.exp(tl_dst[slot]) * carried + t_dst[slot].astype(F32)
        carried = jnp.where(slot < own_group, grown, carried)
    for slot in range(row):
        r_src[slot] = (scan_buf[slot] + jnp.exp(cum_buf[slot]) * carried).astype(BF16)

    def r_copy(k):
        other = (pos + k) % row
        return pltpu.make_async_remote_copy(
            r_src.at[slot_of(other, row, core)],
            r_dst.at[pos],
            r_send.at[k],
            r_recv.at[pos],
            (base + other, hx),
            MESH,
        )

    def r_start(k, carry):
        r_copy(k).start()
        return carry

    lax.fori_loop(1, row, r_start, 0)
    r_dst[pos] = r_src[own_slot]

    for copy in near:
        copy.wait_recv()
    columns = rows
    query_pos = (first + iota((rows, columns), 0)).astype(F32)
    start_wide = jnp.broadcast_to(start_column, (rows, columns))
    masks = []
    for distance in range(3):
        key_pos = (first - distance * rows + iota((rows, columns), 1)).astype(F32)
        masks.append((key_pos >= start_wide) & (key_pos <= query_pos))
    lane = iota((rows, 128), 1)
    stats = jnp.where(lane == 4, start_column, 0.0)
    for h in range(2):
        cols = slice(h * HEAD_DIM, (h + 1) * HEAD_DIM)
        query, grad = q_ref[:, cols], do_ref[:, cols]
        keys = [k_ref[:, cols], kv_in[0, 0, :, cols], kv_in[1, 0, :, cols]]
        values = [v_ref[:, cols], kv_in[0, 1, :, cols], kv_in[1, 1, :, cols]]
        scores = [
            jnp.where(mask, dot_nt(query, key) * SCALE, OFF) for mask, key in zip(masks, keys)
        ]
        top = jnp.max(
            jnp.maximum(jnp.maximum(scores[0], scores[1]), scores[2]), axis=1, keepdims=True
        )
        powers = [jnp.exp(score - top) for score in scores]
        total = jnp.sum(powers[0] + powers[1] + powers[2], axis=1, keepdims=True)
        inverse = 1.0 / total
        probs = [power * inverse for power in powers]
        out = sum(dot(prob.astype(BF16), value) for prob, value in zip(probs, values))
        out = out.astype(BF16)
        attn_ref[:, cols] = out
        delta = jnp.sum(grad.astype(F32) * out.astype(F32), axis=1, keepdims=True)
        slopes = [
            (prob * (dot_nt(grad, value) - delta) * SCALE).astype(BF16)
            for prob, value in zip(probs, values)
        ]
        dq_ref[:, cols] = sum(dot(slope, key) for slope, key in zip(slopes, keys)).astype(BF16)
        stats = jnp.where(lane == h, top + jnp.log(total), stats)
        stats = jnp.where(lane == 2 + h, delta, stats)
    stat_out[...] = stats.T[0:8, :]
    stat_copies = [
        pltpu.make_async_remote_copy(
            stat_out,
            stat_in.at[distance - 1],
            stat_send.at[distance - 1],
            stat_recv.at[distance - 1],
            (seq_at(-distance), hx),
            MESH,
        )
        for distance in (1, 2)
    ]
    for copy in stat_copies:
        copy.start()

    def r_wait(k, carry):
        other = (pos + k) % row
        pltpu.make_async_remote_copy(
            r_src.at[0], r_dst.at[other], r_send.at[k], r_recv.at[other], (me, hx), MESH
        ).wait_recv()
        return carry

    lax.fori_loop(1, row, r_wait, 0)
    for z in range(n_z):
        part = slice(z * width, (z + 1) * width)
        state_ref[hx, 0, part, :] = r_dst[2 * z]
        state_ref[hx, 1, part, :] = (decay_all * r_dst[2 * z + 1].astype(F32)).astype(BF16)
    state_copies = over_head(state_ref, state_send, state_recv)
    for copy in state_copies:
        copy.start()
    y_ref[...] = (
        carry_weight * (y_inner + dot(c_ref[...], state_ref[hx, 0]))
        + gain_wide * x_ref[...].astype(F32)
    ).astype(BF16)
    xg_ref[...] = (
        source_weight * (x_inner + dot(b_ref[...], state_ref[hx, 1]))
        + gain_wide * g_ref[...].astype(F32)
    ).astype(BF16)

    for copy in stat_copies:
        copy.wait_recv()
    key_pos = (first + iota((rows, columns), 0)).astype(F32)
    turned = []
    for distance in range(3):
        stat = stat_out if distance == 0 else stat_in.at[distance - 1]
        query_pos = (seq_at(distance) * rows + iota((rows, columns), 1)).astype(F32)
        turned.append((key_pos >= stat[4:5, :]) & (key_pos <= query_pos))
    for h in range(2):
        cols = slice(h * HEAD_DIM, (h + 1) * HEAD_DIM)
        key, value = k_ref[:, cols], v_ref[:, cols]
        key_total = value_total = jnp.zeros((rows, HEAD_DIM), F32)
        for distance in range(3):
            if distance == 0:
                stat, query, grad = stat_out, q_ref[:, cols], do_ref[:, cols]
            else:
                stat = stat_in.at[distance - 1]
                query, grad = qd_in[distance - 1, 0, :, cols], qd_in[distance - 1, 1, :, cols]
            score = jnp.where(turned[distance], dot_nt(key, query) * SCALE, OFF)
            prob = jnp.exp(score - stat[h : h + 1, :])
            value_total = value_total + dot(prob.astype(BF16), grad)
            slope = prob * (dot_nt(value, grad) - stat[2 + h : 3 + h, :]) * SCALE
            key_total = key_total + dot(slope.astype(BF16), query)
        dk_ref[:, cols] = key_total.astype(BF16)
        dv_ref[:, cols] = value_total.astype(BF16)

    from_head(mix_ref, mix_send, mix_recv)
    from_head(state_ref, state_send, state_recv)

    for copy in near + mix_copies + state_copies + stat_copies:
        copy.wait_send()

    def row_sent(k, carry):
        for copy in (*a_copies(k), r_copy(k)):
            copy.wait_send()
        return carry

    lax.fori_loop(1, row, row_sent, 0)

    def group_sent(k, carry):
        for copy in t_copies(k):
            copy.wait_send()
        return carry

    lax.fori_loop(1, n_y, group_sent, 0)


def last_kernel(
    n_head,
    b_ref,
    c_ref,
    mix_ref,
    state_ref,
    attn_in,
    dq_in,
    dk_in,
    dv_in,
    y_in,
    xg_in,
    attn_ref,
    dq_ref,
    dk_ref,
    dv_ref,
    y_ref,
    xg_ref,
    bg_ref,
    cg_ref,
):
    rows = b_ref.shape[0]
    causal = lower(rows)
    anti = iota((rows, rows), 0) <= iota((rows, rows), 1)
    meet = sum(dot_nt(mix_ref[h, 0], mix_ref[h, 1]) for h in range(n_head))
    meet = jnp.where(causal, meet, 0.0).astype(BF16)
    cg_ref[...] = dot(meet, b_ref[...]) + sum(
        dot_nt(mix_ref[h, 0], state_ref[h, 0]) for h in range(n_head)
    )
    meet = sum(dot_nt(mix_ref[h, 1], mix_ref[h, 0]) for h in range(n_head))
    meet = jnp.where(anti, meet, 0.0).astype(BF16)
    bg_ref[...] = dot(meet, c_ref[...]) + sum(
        dot_nt(mix_ref[h, 1], state_ref[h, 1]) for h in range(n_head)
    )
    for source, target in (
        (attn_in, attn_ref),
        (dq_in, dq_ref),
        (dk_in, dk_ref),
        (dv_in, dv_ref),
        (y_in, y_ref),
        (xg_in, xg_ref),
    ):
        target[...] = source[...]


def on_device(
    n_seq,
    n_head,
    n_z,
    queries,
    key_rows,
    value_rows,
    attn_out_grad,
    ssm_input,
    b_matrix,
    c_matrix,
    step_sizes,
    decay_rates,
    skip_gain,
    ssm_out_grad,
    doc_lengths,
):
    rows, columns = queries.shape
    row, n_y, width = 2 * n_z, n_seq // (2 * n_z), rows // n_z
    vmem = pl.BlockSpec(memory_space=pltpu.VMEM)
    smem = pl.BlockSpec(memory_space=pltpu.SMEM)
    wide = jax.ShapeDtypeStruct((rows, columns), BF16)
    narrow = jax.ShapeDtypeStruct((rows, 128), BF16)
    stacked = jax.ShapeDtypeStruct((n_head, 2, rows, 128), BF16)
    dma = pltpu.SemaphoreType.DMA
    attn, dq, dk, dv, y, xg, mix, state = pl.pallas_call(
        functools.partial(main_kernel, n_seq, n_head, n_z),
        out_shape=(wide, wide, wide, wide, narrow, narrow, stacked, stacked),
        in_specs=[smem, smem] + [vmem] * 10,
        out_specs=(vmem,) * 8,
        scratch_shapes=[
            pltpu.VMEM((2, 2, rows, columns), BF16),
            pltpu.VMEM((2, 2, rows, columns), BF16),
            pltpu.VMEM((8, rows), F32),
            pltpu.VMEM((2, 8, rows), F32),
            pltpu.VMEM((row, width, 128), BF16),
            pltpu.VMEM((row, width, 128), BF16),
            pltpu.VMEM((1, 128), F32),
            pltpu.VMEM((row, 1, 128), F32),
            pltpu.VMEM((row, width, 128), F32),
            pltpu.VMEM((row, 1, 128), F32),
            pltpu.VMEM((width, 128), BF16),
            pltpu.VMEM((n_y, width, 128), BF16),
            pltpu.VMEM((1, 128), F32),
            pltpu.VMEM((n_y, 1, 128), F32),
            pltpu.VMEM((row, width, 128), BF16),
            pltpu.VMEM((row, width, 128), BF16),
            dma((8,)),
            dma((8,)),
            dma((2,)),
            dma((2,)),
            dma((row,)),
            dma((row,)),
            dma((row,)),
            dma((row,)),
            dma((n_y,)),
            dma((n_y,)),
            dma((n_y,)),
            dma((n_y,)),
            dma((row,)),
            dma((row,)),
            dma((n_head,)),
            dma((n_head,)),
            dma((n_head,)),
            dma((n_head,)),
        ],
        compiler_params=pltpu.CompilerParams(
            collective_id=0, has_side_effects=True, vmem_limit_bytes=VMEM_BYTES
        ),
        name="main",
    )(
        decay_rates,
        skip_gain,
        doc_lengths.reshape(1, -1),
        queries,
        key_rows,
        value_rows,
        attn_out_grad,
        ssm_input,
        ssm_out_grad,
        b_matrix,
        c_matrix,
        step_sizes.T,
    )
    grads = jax.ShapeDtypeStruct((rows, b_matrix.shape[1]), F32)
    return pl.pallas_call(
        functools.partial(last_kernel, n_head),
        out_shape=(wide, wide, wide, wide, narrow, narrow, grads, grads),
        in_specs=[vmem] * 10,
        out_specs=(vmem,) * 8,
        compiler_params=pltpu.CompilerParams(vmem_limit_bytes=VMEM_BYTES),
        name="last",
    )(b_matrix, c_matrix, mix, state, attn, dq, dk, dv, y, xg)


def build(mesh, n_z):
    n_seq, n_head = mesh.shape["seq"], mesh.shape["head"]
    tokens = P("seq", "head")
    whole = P("seq", None)
    return jax.shard_map(
        functools.partial(on_device, n_seq, n_head, n_z),
        mesh=mesh,
        in_specs=(
            tokens,
            tokens,
            tokens,
            tokens,
            tokens,
            whole,
            whole,
            tokens,
            P("head"),
            P("head"),
            tokens,
            P(),
        ),
        out_specs=(tokens, tokens, tokens, tokens, tokens, tokens, whole, whole),
        check_vma=False,
    )


def solution(mesh):
    return build(mesh, 8)
```

```python
import functools

import jax
import jax.numpy as jnp
from jax import lax
from jax.experimental import pallas as pl
from jax.experimental.pallas import tpu as pltpu
from jax.sharding import PartitionSpec as P

MESH = pl.DeviceIdType.MESH
HEAD_DIM = 128
SCALE = HEAD_DIM**-0.5
OFF = -1e30
F32 = jnp.float32
BF16 = jnp.bfloat16
UNROLL = False
NEAR_AT = 3
VMEM_BYTES = 60 * 1024 * 1024


def far_first(step, count):
    odd = step % 2
    return count // 2 + (step // 2 + odd) * (1 - 2 * odd)


def dot(a, b):
    return jnp.dot(a, b, preferred_element_type=F32)


def dot_nt(a, b):
    return lax.dot_general(a, b, (((1,), (1,)), ((), ())), preferred_element_type=F32)


def dot_tn(a, b):
    return lax.dot_general(a, b, (((0,), (0,)), ((), ())), preferred_element_type=F32)


def iota(shape, axis):
    return lax.broadcasted_iota(jnp.int32, shape, axis)


def lower(size):
    return iota((size, size), 1) <= iota((size, size), 0)


def doc_start_column(doc_ref, first, rows):
    docs = doc_ref.shape[1]
    lengths = jnp.broadcast_to(doc_ref[...], (16, docs))
    upper = jnp.where(iota((docs, docs), 0) <= iota((docs, docs), 1), 1.0, 0.0).astype(BF16)
    high, low = lengths // 16, lengths % 16
    ends = 16.0 * dot(high.astype(F32).astype(BF16), upper) + dot(
        low.astype(F32).astype(BF16), upper
    )
    ends = jnp.broadcast_to(ends[0:1, :], (rows, docs))
    position = (first + iota((rows, docs), 0)).astype(F32)
    return jnp.max(jnp.where(ends <= position, ends, 0.0), axis=1, keepdims=True)


def running_sum(rows):
    ones = jnp.where(lower(rows.shape[0]), 1.0, 0.0).astype(BF16)
    high = rows.astype(BF16)
    rest = rows - high.astype(F32)
    middle = rest.astype(BF16)
    low = (rest - middle.astype(F32)).astype(BF16)
    return dot(ones, high) + dot(ones, middle) + dot(ones, low)


def main_kernel(
    n_seq,
    n_head,
    n_z,
    rate_ref,
    gain_ref,
    doc_ref,
    dt_ref,
    q_hbm,
    k_hbm,
    v_hbm,
    do_hbm,
    x_hbm,
    g_hbm,
    b_hbm,
    c_hbm,
    attn_ref,
    dq_ref,
    dk_ref,
    dv_ref,
    y_ref,
    xg_ref,
    mix_ref,
    state_ref,
    q_ref,
    k_ref,
    v_ref,
    do_ref,
    x_ref,
    g_ref,
    b_ref,
    c_ref,
    load_sem,
    kv_in,
    qd_in,
    stat_out,
    stat_in,
    a_src,
    a_dst,
    la_src,
    la_dst,
    scan_buf,
    cum_buf,
    t_src,
    t_dst,
    tl_src,
    tl_dst,
    r_src,
    r_dst,
    near_send,
    near_recv,
    stat_send,
    stat_recv,
    a_send,
    a_recv,
    la_send,
    la_recv,
    t_send,
    t_recv,
    tl_send,
    tl_recv,
    r_send,
    r_recv,
    mix_send,
    mix_recv,
    state_send,
    state_recv,
):
    me = lax.axis_index("seq")
    hx = lax.axis_index("head")
    row = 2 * n_z
    n_y = n_seq // row
    rows = q_ref.shape[0]
    group, pos = me // row, me % row
    core = pos % 2
    base = group * row
    width = rows // n_z

    def seq_at(offset):
        return (me + offset + n_seq) % n_seq

    def slot_of(index, count, side):
        return index + side * (count - 1 - 2 * index)

    loads = [
        pltpu.make_async_copy(source, target, load_sem.at[at])
        for at, (source, target) in enumerate(
            (
                (x_hbm, x_ref),
                (b_hbm, b_ref),
                (g_hbm, g_ref),
                (c_hbm, c_ref),
                (q_hbm, q_ref),
                (k_hbm, k_ref),
                (v_hbm, v_ref),
                (do_hbm, do_ref),
            )
        )
    ]
    for load in loads:
        load.start()

    barrier = pltpu.get_barrier_semaphore()

    def greet(seq_index, head_index):
        pl.semaphore_signal(
            barrier, inc=1, device_id=(seq_index, head_index), device_id_type=MESH
        )

    for offset in (-2, -1, 1, 2):
        greet(seq_at(offset), hx)

    def greet_row(k, carry):
        greet(base + (pos + k) % row, hx)
        return carry

    lax.fori_loop(1, row, greet_row, 0)

    def greet_group(k, carry):
        greet(((group + k) % n_y) * row + pos, hx)
        return carry

    lax.fori_loop(1, n_y, greet_group, 0)
    for k in range(1, n_head):
        greet(me, (hx + k) % n_head)

    lanes_low = iota((rows, 128), 1) < 64
    dt_wide = jnp.concatenate(
        [
            jnp.broadcast_to(dt_ref[0:1, :], (64, rows)),
            jnp.broadcast_to(dt_ref[1:2, :], (64, rows)),
        ],
        axis=0,
    ).T
    rate_wide = jnp.where(lanes_low, rate_ref[0], rate_ref[1])
    gain_wide = jnp.where(lanes_low, gain_ref[0], gain_ref[1])
    log_decay = running_sum(-dt_wide * rate_wide)
    carry_weight = jnp.exp(log_decay)
    source_weight = jnp.exp(-log_decay) * dt_wide
    last = log_decay[rows - 1 : rows, :]
    decay_all = jnp.exp(last)
    for load in loads[:4]:
        load.wait()
    mix_ref[hx, 0] = (carry_weight * g_ref[...].astype(F32)).astype(BF16)
    mix_ref[hx, 1] = (source_weight * x_ref[...].astype(F32)).astype(BF16)
    local_state = (decay_all * dot_tn(b_ref[...], mix_ref[hx, 1])).astype(BF16)
    local_adjoint = dot_tn(c_ref[...], mix_ref[hx, 0]).astype(BF16)
    for z in range(n_z):
        a_src[2 * z] = local_state[z * width : (z + 1) * width, :]
        a_src[2 * z + 1] = local_adjoint[z * width : (z + 1) * width, :]
    la_src[...] = last

    pl.semaphore_wait(barrier, 4 + (row - 1) + (n_y - 1) + (n_head - 1))

    def a_copies(k):
        owner = (pos + k) % row
        slot = slot_of(pos, row, owner % 2)
        target = (base + owner, hx)
        return (
            pltpu.make_async_remote_copy(
                a_src.at[owner], a_dst.at[slot], a_send.at[k], a_recv.at[slot], target, MESH
            ),
            pltpu.make_async_remote_copy(
                la_src, la_dst.at[slot], la_send.at[k], la_recv.at[slot], target, MESH
            ),
        )

    def a_start(step, carry):
        for copy in a_copies(far_first(step, row)):
            copy.start()
        return carry

    lax.fori_loop(0, row - 1, a_start, 0, unroll=UNROLL)
    own_slot = slot_of(pos, row, core)
    a_dst[own_slot] = a_src[pos]
    la_dst[own_slot] = la_src[...]

    near = []
    for distance in (1, 2):
        for part, (fore, back) in enumerate(((k_hbm, q_hbm), (v_hbm, do_hbm))):
            at = (distance - 1) * 2 + part
            near.append(
                pltpu.make_async_remote_copy(
                    fore,
                    kv_in.at[distance - 1, part],
                    near_send.at[at],
                    near_recv.at[at],
                    (seq_at(distance), hx),
                    MESH,
                )
            )
            near.append(
                pltpu.make_async_remote_copy(
                    back,
                    qd_in.at[distance - 1, part],
                    near_send.at[4 + at],
                    near_recv.at[4 + at],
                    (seq_at(-distance), hx),
                    MESH,
                )
            )
    if NEAR_AT == 1:
        for copy in near:
            copy.start()

    def over_head(ref, send, recv):
        return [
            pltpu.make_async_remote_copy(
                ref.at[hx],
                ref.at[hx],
                send.at[k],
                recv.at[hx],
                (me, (hx + k) % n_head),
                MESH,
            )
            for k in [far_first(step, n_head) for step in range(n_head - 1)]
        ]

    def from_head(ref, send, recv):
        for k in range(1, n_head):
            other = (hx + k) % n_head
            pltpu.make_async_remote_copy(
                ref.at[hx], ref.at[other], send.at[k], recv.at[other], (me, other), MESH
            ).wait_recv()

    mix_copies = over_head(mix_ref, mix_send, mix_recv)
    for copy in mix_copies:
        copy.start()

    causal = lower(rows)
    meet = jnp.where(causal, dot_nt(c_ref[...], b_ref[...]), 0.0).astype(BF16)
    y_inner = dot(meet, mix_ref[hx, 1])
    meet_back = jnp.where(
        iota((rows, rows), 0) <= iota((rows, rows), 1), dot_nt(b_ref[...], c_ref[...]), 0.0
    ).astype(BF16)
    x_inner = dot(meet_back, mix_ref[hx, 0])

    def a_wait(k, carry):
        slot = (own_slot + k) % row
        pltpu.make_async_remote_copy(
            a_src.at[0], a_dst.at[slot], a_send.at[k], a_recv.at[slot], (me, hx), MESH
        ).wait_recv()
        pltpu.make_async_remote_copy(
            la_src, la_dst.at[slot], la_send.at[k], la_recv.at[slot], (me, hx), MESH
        ).wait_recv()
        return carry

    lax.fori_loop(1, row, a_wait, 0)
    if NEAR_AT == 2:
        for copy in near:
            copy.start()

    state = jnp.zeros((width, 128), F32)
    summed = jnp.zeros((1, 128), F32)
    for slot in range(row):
        scan_buf[slot] = state
        cum_buf[slot] = summed
        state = jnp.exp(la_dst[slot]) * state + a_dst[slot].astype(F32)
        summed = summed + la_dst[slot]
    t_src[...] = state.astype(BF16)
    tl_src[...] = summed

    own_group = slot_of(group, n_y, core)

    def t_copies(k):
        target = (((group + k) % n_y) * row + pos, hx)
        return (
            pltpu.make_async_remote_copy(
                t_src, t_dst.at[own_group], t_send.at[k], t_recv.at[own_group], target, MESH
            ),
            pltpu.make_async_remote_copy(
                tl_src, tl_dst.at[own_group], tl_send.at[k], tl_recv.at[own_group], target, MESH
            ),
        )

    def t_start(step, carry):
        for copy in t_copies(far_first(step, n_y)):
            copy.start()
        return carry

    lax.fori_loop(0, n_y - 1, t_start, 0, unroll=UNROLL)
    if NEAR_AT == 3:
        for copy in near:
            copy.start()
    t_dst[own_group] = t_src[...]
    tl_dst[own_group] = tl_src[...]

    first = me * rows
    start_column = doc_start_column(doc_ref, first, rows)

    def t_wait(k, carry):
        slot = (own_group + k) % n_y
        pltpu.make_async_remote_copy(
            t_src, t_dst.at[slot], t_send.at[k], t_recv.at[slot], (me, hx), MESH
        ).wait_recv()
        pltpu.make_async_remote_copy(
            tl_src, tl_dst.at[slot], tl_send.at[k], tl_recv.at[slot], (me, hx), MESH
        ).wait_recv()
        return carry

    lax.fori_loop(1, n_y, t_wait, 0)
    carried = jnp.zeros((width, 128), F32)
    for slot in range(n_y):
        grown = jnp.exp(tl_dst[slot]) * carried + t_dst[slot].astype(F32)
        carried = jnp.where(slot < own_group, grown, carried)
    for slot in range(row):
        r_src[slot] = (scan_buf[slot] + jnp.exp(cum_buf[slot]) * carried).astype(BF16)

    def r_copy(k):
        other = (pos + k) % row
        return pltpu.make_async_remote_copy(
            r_src.at[slot_of(other, row, core)],
            r_dst.at[pos],
            r_send.at[k],
            r_recv.at[pos],
            (base + other, hx),
            MESH,
        )

    def r_start(step, carry):
        r_copy(far_first(step, row)).start()
        return carry

    lax.fori_loop(0, row - 1, r_start, 0, unroll=UNROLL)
    r_dst[pos] = r_src[own_slot]

    for load in loads[4:]:
        load.wait()
    for copy in near:
        copy.wait_recv()
    columns = rows
    query_pos = (first + iota((rows, columns), 0)).astype(F32)
    start_wide = jnp.broadcast_to(start_column, (rows, columns))
    masks = []
    for distance in range(3):
        key_pos = (first - distance * rows + iota((rows, columns), 1)).astype(F32)
        masks.append((key_pos >= start_wide) & (key_pos <= query_pos))
    lane = iota((rows, 128), 1)
    stats = jnp.where(lane == 4, start_column, 0.0)
    for h in range(2):
        cols = slice(h * HEAD_DIM, (h + 1) * HEAD_DIM)
        query, grad = q_ref[:, cols], do_ref[:, cols]
        keys = [k_ref[:, cols], kv_in[0, 0, :, cols], kv_in[1, 0, :, cols]]
        values = [v_ref[:, cols], kv_in[0, 1, :, cols], kv_in[1, 1, :, cols]]
        scores = [
            jnp.where(mask, dot_nt(query, key) * SCALE, OFF) for mask, key in zip(masks, keys)
        ]
        top = jnp.max(
            jnp.maximum(jnp.maximum(scores[0], scores[1]), scores[2]), axis=1, keepdims=True
        )
        powers = [jnp.exp(score - top) for score in scores]
        total = jnp.sum(powers[0] + powers[1] + powers[2], axis=1, keepdims=True)
        inverse = 1.0 / total
        probs = [power * inverse for power in powers]
        out = sum(dot(prob.astype(BF16), value) for prob, value in zip(probs, values))
        out = out.astype(BF16)
        attn_ref[:, cols] = out
        delta = jnp.sum(grad.astype(F32) * out.astype(F32), axis=1, keepdims=True)
        slopes = [
            (prob * (dot_nt(grad, value) - delta) * SCALE).astype(BF16)
            for prob, value in zip(probs, values)
        ]
        dq_ref[:, cols] = sum(dot(slope, key) for slope, key in zip(slopes, keys)).astype(BF16)
        stats = jnp.where(lane == h, top + jnp.log(total), stats)
        stats = jnp.where(lane == 2 + h, delta, stats)
    stat_out[...] = stats.T[0:8, :]
    stat_copies = [
        pltpu.make_async_remote_copy(
            stat_out,
            stat_in.at[distance - 1],
            stat_send.at[distance - 1],
            stat_recv.at[distance - 1],
            (seq_at(-distance), hx),
            MESH,
        )
        for distance in (1, 2)
    ]
    for copy in stat_copies:
        copy.start()

    def r_wait(k, carry):
        other = (pos + k) % row
        pltpu.make_async_remote_copy(
            r_src.at[0], r_dst.at[other], r_send.at[k], r_recv.at[other], (me, hx), MESH
        ).wait_recv()
        return carry

    lax.fori_loop(1, row, r_wait, 0)
    for z in range(n_z):
        part = slice(z * width, (z + 1) * width)
        state_ref[hx, 0, part, :] = r_dst[2 * z]
        state_ref[hx, 1, part, :] = (decay_all * r_dst[2 * z + 1].astype(F32)).astype(BF16)
    state_copies = over_head(state_ref, state_send, state_recv)
    for copy in state_copies:
        copy.start()
    y_ref[...] = (
        carry_weight * (y_inner + dot(c_ref[...], state_ref[hx, 0]))
        + gain_wide * x_ref[...].astype(F32)
    ).astype(BF16)
    xg_ref[...] = (
        source_weight * (x_inner + dot(b_ref[...], state_ref[hx, 1]))
        + gain_wide * g_ref[...].astype(F32)
    ).astype(BF16)

    for copy in stat_copies:
        copy.wait_recv()
    key_pos = (first + iota((rows, columns), 0)).astype(F32)
    turned = []
    for distance in range(3):
        stat = stat_out if distance == 0 else stat_in.at[distance - 1]
        query_pos = (seq_at(distance) * rows + iota((rows, columns), 1)).astype(F32)
        turned.append((key_pos >= stat[4:5, :]) & (key_pos <= query_pos))
    for h in range(2):
        cols = slice(h * HEAD_DIM, (h + 1) * HEAD_DIM)
        key, value = k_ref[:, cols], v_ref[:, cols]
        key_total = value_total = jnp.zeros((rows, HEAD_DIM), F32)
        for distance in range(3):
            if distance == 0:
                stat, query, grad = stat_out, q_ref[:, cols], do_ref[:, cols]
            else:
                stat = stat_in.at[distance - 1]
                query, grad = qd_in[distance - 1, 0, :, cols], qd_in[distance - 1, 1, :, cols]
            score = jnp.where(turned[distance], dot_nt(key, query) * SCALE, OFF)
            prob = jnp.exp(score - stat[h : h + 1, :])
            value_total = value_total + dot(prob.astype(BF16), grad)
            slope = prob * (dot_nt(value, grad) - stat[2 + h : 3 + h, :]) * SCALE
            key_total = key_total + dot(slope.astype(BF16), query)
        dk_ref[:, cols] = key_total.astype(BF16)
        dv_ref[:, cols] = value_total.astype(BF16)

    from_head(mix_ref, mix_send, mix_recv)
    from_head(state_ref, state_send, state_recv)

    for copy in near + mix_copies + state_copies + stat_copies:
        copy.wait_send()

    def row_sent(k, carry):
        for copy in (*a_copies(k), r_copy(k)):
            copy.wait_send()
        return carry

    lax.fori_loop(1, row, row_sent, 0)

    def group_sent(k, carry):
        for copy in t_copies(k):
            copy.wait_send()
        return carry

    lax.fori_loop(1, n_y, group_sent, 0)


def last_kernel(
    n_head,
    b_ref,
    c_ref,
    mix_ref,
    state_ref,
    attn_in,
    dq_in,
    dk_in,
    dv_in,
    y_in,
    xg_in,
    attn_ref,
    dq_ref,
    dk_ref,
    dv_ref,
    y_ref,
    xg_ref,
    bg_ref,
    cg_ref,
):
    rows = b_ref.shape[0]
    causal = lower(rows)
    anti = iota((rows, rows), 0) <= iota((rows, rows), 1)
    meet = sum(dot_nt(mix_ref[h, 0], mix_ref[h, 1]) for h in range(n_head))
    meet = jnp.where(causal, meet, 0.0).astype(BF16)
    cg_ref[...] = dot(meet, b_ref[...]) + sum(
        dot_nt(mix_ref[h, 0], state_ref[h, 0]) for h in range(n_head)
    )
    meet = sum(dot_nt(mix_ref[h, 1], mix_ref[h, 0]) for h in range(n_head))
    meet = jnp.where(anti, meet, 0.0).astype(BF16)
    bg_ref[...] = dot(meet, c_ref[...]) + sum(
        dot_nt(mix_ref[h, 1], state_ref[h, 1]) for h in range(n_head)
    )
    for source, target in (
        (attn_in, attn_ref),
        (dq_in, dq_ref),
        (dk_in, dk_ref),
        (dv_in, dv_ref),
        (y_in, y_ref),
        (xg_in, xg_ref),
    ):
        target[...] = source[...]


def on_device(
    n_seq,
    n_head,
    n_z,
    queries,
    key_rows,
    value_rows,
    attn_out_grad,
    ssm_input,
    b_matrix,
    c_matrix,
    step_sizes,
    decay_rates,
    skip_gain,
    ssm_out_grad,
    doc_lengths,
):
    rows, columns = queries.shape
    row, n_y, width = 2 * n_z, n_seq // (2 * n_z), rows // n_z
    vmem = pl.BlockSpec(memory_space=pltpu.VMEM)
    smem = pl.BlockSpec(memory_space=pltpu.SMEM)
    wide = jax.ShapeDtypeStruct((rows, columns), BF16)
    narrow = jax.ShapeDtypeStruct((rows, 128), BF16)
    stacked = jax.ShapeDtypeStruct((n_head, 2, rows, 128), BF16)
    dma = pltpu.SemaphoreType.DMA
    attn, dq, dk, dv, y, xg, mix, state = pl.pallas_call(
        functools.partial(main_kernel, n_seq, n_head, n_z),
        out_shape=(wide, wide, wide, wide, narrow, narrow, stacked, stacked),
        in_specs=[smem, smem] + [vmem] * 2 + [pl.BlockSpec(memory_space=pltpu.HBM)] * 8,
        out_specs=(vmem,) * 8,
        scratch_shapes=[
            pltpu.VMEM((rows, columns), BF16),
            pltpu.VMEM((rows, columns), BF16),
            pltpu.VMEM((rows, columns), BF16),
            pltpu.VMEM((rows, columns), BF16),
            pltpu.VMEM((rows, 128), BF16),
            pltpu.VMEM((rows, 128), BF16),
            pltpu.VMEM((rows, b_matrix.shape[1]), BF16),
            pltpu.VMEM((rows, b_matrix.shape[1]), BF16),
            dma((8,)),
            pltpu.VMEM((2, 2, rows, columns), BF16),
            pltpu.VMEM((2, 2, rows, columns), BF16),
            pltpu.VMEM((8, rows), F32),
            pltpu.VMEM((2, 8, rows), F32),
            pltpu.VMEM((row, width, 128), BF16),
            pltpu.VMEM((row, width, 128), BF16),
            pltpu.VMEM((1, 128), F32),
            pltpu.VMEM((row, 1, 128), F32),
            pltpu.VMEM((row, width, 128), F32),
            pltpu.VMEM((row, 1, 128), F32),
            pltpu.VMEM((width, 128), BF16),
            pltpu.VMEM((n_y, width, 128), BF16),
            pltpu.VMEM((1, 128), F32),
            pltpu.VMEM((n_y, 1, 128), F32),
            pltpu.VMEM((row, width, 128), BF16),
            pltpu.VMEM((row, width, 128), BF16),
            dma((8,)),
            dma((8,)),
            dma((2,)),
            dma((2,)),
            dma((row,)),
            dma((row,)),
            dma((row,)),
            dma((row,)),
            dma((n_y,)),
            dma((n_y,)),
            dma((n_y,)),
            dma((n_y,)),
            dma((row,)),
            dma((row,)),
            dma((n_head,)),
            dma((n_head,)),
            dma((n_head,)),
            dma((n_head,)),
        ],
        compiler_params=pltpu.CompilerParams(
            collective_id=0, has_side_effects=True, vmem_limit_bytes=VMEM_BYTES
        ),
        name="main",
    )(
        decay_rates,
        skip_gain,
        doc_lengths.reshape(1, -1),
        step_sizes.T,
        queries,
        key_rows,
        value_rows,
        attn_out_grad,
        ssm_input,
        ssm_out_grad,
        b_matrix,
        c_matrix,
    )
    grads = jax.ShapeDtypeStruct((rows, b_matrix.shape[1]), F32)
    return pl.pallas_call(
        functools.partial(last_kernel, n_head),
        out_shape=(wide, wide, wide, wide, narrow, narrow, grads, grads),
        in_specs=[vmem] * 10,
        out_specs=(vmem,) * 8,
        compiler_params=pltpu.CompilerParams(vmem_limit_bytes=VMEM_BYTES),
        name="last",
    )(b_matrix, c_matrix, mix, state, attn, dq, dk, dv, y, xg)


def build(mesh, n_z):
    n_seq, n_head = mesh.shape["seq"], mesh.shape["head"]
    tokens = P("seq", "head")
    whole = P("seq", None)
    return jax.shard_map(
        functools.partial(on_device, n_seq, n_head, n_z),
        mesh=mesh,
        in_specs=(
            tokens,
            tokens,
            tokens,
            tokens,
            tokens,
            whole,
            whole,
            tokens,
            P("head"),
            P("head"),
            tokens,
            P(),
        ),
        out_specs=(tokens, tokens, tokens, tokens, tokens, tokens, whole, whole),
        check_vma=False,
    )


def solution(mesh):
    return build(mesh, 8)
```

```python
import functools

import jax
import jax.numpy as jnp
from jax import lax
from jax.experimental import pallas as pl
from jax.experimental.pallas import tpu as pltpu
from jax.sharding import PartitionSpec as P

MESH = pl.DeviceIdType.MESH
HEAD_DIM = 128
SCALE = HEAD_DIM**-0.5
OFF = -1e30
F32 = jnp.float32
BF16 = jnp.bfloat16
UNROLL = False
NEAR_AT = 1
VMEM_BYTES = 40 * 1024 * 1024


def far_first(step, count):
    odd = step % 2
    return count // 2 + (step // 2 + odd) * (1 - 2 * odd)


def dot(a, b):
    return jnp.dot(a, b, preferred_element_type=F32)


def dot_nt(a, b):
    return lax.dot_general(a, b, (((1,), (1,)), ((), ())), preferred_element_type=F32)


def dot_tn(a, b):
    return lax.dot_general(a, b, (((0,), (0,)), ((), ())), preferred_element_type=F32)


def iota(shape, axis):
    return lax.broadcasted_iota(jnp.int32, shape, axis)


def lower(size):
    return iota((size, size), 1) <= iota((size, size), 0)


def doc_start_column(doc_ref, first, rows):
    docs = doc_ref.shape[1]
    lengths = jnp.broadcast_to(doc_ref[...], (16, docs))
    upper = jnp.where(iota((docs, docs), 0) <= iota((docs, docs), 1), 1.0, 0.0).astype(BF16)
    high, low = lengths // 16, lengths % 16
    ends = 16.0 * dot(high.astype(F32).astype(BF16), upper) + dot(
        low.astype(F32).astype(BF16), upper
    )
    ends = jnp.broadcast_to(ends[0:1, :], (rows, docs))
    position = (first + iota((rows, docs), 0)).astype(F32)
    return jnp.max(jnp.where(ends <= position, ends, 0.0), axis=1, keepdims=True)


def running_sum(rows):
    ones = jnp.where(lower(rows.shape[0]), 1.0, 0.0).astype(BF16)
    high = rows.astype(BF16)
    rest = rows - high.astype(F32)
    middle = rest.astype(BF16)
    low = (rest - middle.astype(F32)).astype(BF16)
    return dot(ones, high) + dot(ones, middle) + dot(ones, low)


def main_kernel(
    n_seq,
    n_head,
    n_z,
    rate_ref,
    gain_ref,
    doc_ref,
    dt_ref,
    q_hbm,
    k_hbm,
    v_hbm,
    do_hbm,
    x_hbm,
    g_hbm,
    b_hbm,
    c_hbm,
    attn_ref,
    dq_ref,
    dk_ref,
    dv_ref,
    y_ref,
    xg_ref,
    bg_ref,
    cg_ref,
    mix_ref,
    state_ref,
    q_ref,
    k_ref,
    v_ref,
    do_ref,
    x_ref,
    g_ref,
    b_ref,
    c_ref,
    load_sem,
    kv_in,
    qd_in,
    stat_out,
    stat_in,
    a_src,
    a_dst,
    la_src,
    la_dst,
    scan_buf,
    cum_buf,
    t_src,
    t_dst,
    tl_src,
    tl_dst,
    r_src,
    near_send,
    near_recv,
    stat_send,
    stat_recv,
    a_send,
    a_recv,
    la_send,
    la_recv,
    t_send,
    t_recv,
    tl_send,
    tl_recv,
    r_send,
    r_recv,
    mix_send,
    mix_recv,
    state_send,
    state_recv,
):
    me = lax.axis_index("seq")
    hx = lax.axis_index("head")
    row = 2 * n_z
    n_y = n_seq // row
    rows = q_ref.shape[0]
    group, pos = me // row, me % row
    chip, core = pos // 2, pos % 2
    base = group * row
    width = rows // n_z

    def seq_at(offset):
        return (me + offset + n_seq) % n_seq

    def slot_of(index, count, side):
        return index + side * (count - 1 - 2 * index)

    loads = [
        pltpu.make_async_copy(source, target, load_sem.at[at])
        for at, (source, target) in enumerate(
            (
                (x_hbm, x_ref),
                (b_hbm, b_ref),
                (g_hbm, g_ref),
                (c_hbm, c_ref),
                (q_hbm, q_ref),
                (k_hbm, k_ref),
                (v_hbm, v_ref),
                (do_hbm, do_ref),
            )
        )
    ]
    for load in loads:
        load.start()

    barrier = pltpu.get_barrier_semaphore()

    def greet(seq_index, head_index):
        pl.semaphore_signal(
            barrier, inc=1, device_id=(seq_index, head_index), device_id_type=MESH
        )

    for offset in (-2, -1, 1, 2):
        greet(seq_at(offset), hx)

    def greet_row(k, carry):
        greet(base + (pos + k) % row, hx)
        return carry

    lax.fori_loop(1, row, greet_row, 0)

    def greet_group(k, carry):
        greet(((group + k) % n_y) * row + pos, hx)
        return carry

    lax.fori_loop(1, n_y, greet_group, 0)
    for k in range(1, n_head):
        greet(me, (hx + k) % n_head)

    lanes_low = iota((rows, 128), 1) < 64
    dt_wide = jnp.concatenate(
        [
            jnp.broadcast_to(dt_ref[0:1, :], (64, rows)),
            jnp.broadcast_to(dt_ref[1:2, :], (64, rows)),
        ],
        axis=0,
    ).T
    rate_wide = jnp.where(lanes_low, rate_ref[0], rate_ref[1])
    gain_wide = jnp.where(lanes_low, gain_ref[0], gain_ref[1])
    log_decay = running_sum(-dt_wide * rate_wide)
    carry_weight = jnp.exp(log_decay)
    source_weight = jnp.exp(-log_decay) * dt_wide
    last = log_decay[rows - 1 : rows, :]
    decay_all = jnp.exp(last)
    for load in loads[:4]:
        load.wait()
    mix_ref[hx, 0] = (carry_weight * g_ref[...].astype(F32)).astype(BF16)
    mix_ref[hx, 1] = (source_weight * x_ref[...].astype(F32)).astype(BF16)
    local_state = (decay_all * dot_tn(b_ref[...], mix_ref[hx, 1])).astype(BF16)
    local_adjoint = dot_tn(c_ref[...], mix_ref[hx, 0]).astype(BF16)
    for z in range(n_z):
        a_src[2 * z] = local_state[z * width : (z + 1) * width, :]
        a_src[2 * z + 1] = local_adjoint[z * width : (z + 1) * width, :]
    la_src[...] = last

    pl.semaphore_wait(barrier, 4 + (row - 1) + (n_y - 1) + (n_head - 1))

    def a_copies(k):
        owner = (pos + k) % row
        slot = slot_of(pos, row, owner % 2)
        target = (base + owner, hx)
        return (
            pltpu.make_async_remote_copy(
                a_src.at[owner], a_dst.at[slot], a_send.at[k], a_recv.at[slot], target, MESH
            ),
            pltpu.make_async_remote_copy(
                la_src, la_dst.at[slot], la_send.at[k], la_recv.at[slot], target, MESH
            ),
        )

    def a_start(step, carry):
        for copy in a_copies(far_first(step, row)):
            copy.start()
        return carry

    lax.fori_loop(0, row - 1, a_start, 0, unroll=UNROLL)
    own_slot = slot_of(pos, row, core)
    a_dst[own_slot] = a_src[pos]
    la_dst[own_slot] = la_src[...]

    def near_copy(source, place, part, at, offset, sem):
        return pltpu.make_async_remote_copy(
            source,
            place.at[at, part],
            near_send.at[sem],
            near_recv.at[(2 if place is qd_in else 0) + 4 * at + part],
            (seq_at(offset), hx),
            MESH,
        )

    keys_hbm, queries_hbm = (k_hbm, v_hbm), (q_hbm, do_hbm)
    first_copies = [near_copy(keys_hbm[p], kv_in, p, 0, 1, p) for p in (0, 1)]
    first_copies += [near_copy(queries_hbm[p], qd_in, p, 0, -1, 2 + p) for p in (0, 1)]
    far_keys = [near_copy(keys_hbm[p], kv_in, p, 1, 2, 4 + p) for p in (0, 1)]
    far_queries = [near_copy(queries_hbm[p], qd_in, p, 1, -2, 4 + p) for p in (0, 1)]
    pass_keys = [near_copy(kv_in.at[0, p], kv_in, p, 1, 1, 6 + p) for p in (0, 1)]
    pass_queries = [near_copy(qd_in.at[0, p], qd_in, p, 1, -1, 6 + p) for p in (0, 1)]

    def near_start():
        for copy in first_copies:
            copy.start()

        @pl.when(core == 0)
        def _():
            for copy in far_keys:
                copy.start()

        @pl.when(core == 1)
        def _():
            for copy in far_queries:
                copy.start()

    def near_pass():
        for copy in first_copies:
            copy.wait_recv()

        @pl.when(core == 0)
        def _():
            for copy in pass_keys:
                copy.start()

        @pl.when(core == 1)
        def _():
            for copy in pass_queries:
                copy.start()

    if NEAR_AT == 1:
        near_start()

    def mix_copy(k):
        return pltpu.make_async_remote_copy(
            mix_ref.at[hx],
            mix_ref.at[hx],
            mix_send.at[k],
            mix_recv.at[hx],
            (me, (hx + k) % n_head),
            MESH,
        )

    head_steps = [far_first(step, n_head) for step in range(n_head - 1)]
    mix_copies = [mix_copy(k) for k in head_steps]
    for copy in mix_copies:
        copy.start()

    causal = lower(rows)
    meet = jnp.where(causal, dot_nt(c_ref[...], b_ref[...]), 0.0).astype(BF16)
    y_inner = dot(meet, mix_ref[hx, 1])
    meet_back = jnp.where(
        iota((rows, rows), 0) <= iota((rows, rows), 1), dot_nt(b_ref[...], c_ref[...]), 0.0
    ).astype(BF16)
    x_inner = dot(meet_back, mix_ref[hx, 0])

    def a_wait(k, carry):
        slot = (own_slot + k) % row
        pltpu.make_async_remote_copy(
            a_src.at[0], a_dst.at[slot], a_send.at[k], a_recv.at[slot], (me, hx), MESH
        ).wait_recv()
        pltpu.make_async_remote_copy(
            la_src, la_dst.at[slot], la_send.at[k], la_recv.at[slot], (me, hx), MESH
        ).wait_recv()
        return carry

    lax.fori_loop(1, row, a_wait, 0)
    if NEAR_AT == 2:
        near_start()

    state = jnp.zeros((width, 128), F32)
    summed = jnp.zeros((1, 128), F32)
    for slot in range(row):
        scan_buf[slot] = state
        cum_buf[slot] = summed
        state = jnp.exp(la_dst[slot]) * state + a_dst[slot].astype(F32)
        summed = summed + la_dst[slot]
    t_src[...] = state.astype(BF16)
    tl_src[...] = summed

    own_group = slot_of(group, n_y, core)

    def t_copies(k):
        target = (((group + k) % n_y) * row + pos, hx)
        return (
            pltpu.make_async_remote_copy(
                t_src, t_dst.at[own_group], t_send.at[k], t_recv.at[own_group], target, MESH
            ),
            pltpu.make_async_remote_copy(
                tl_src, tl_dst.at[own_group], tl_send.at[k], tl_recv.at[own_group], target, MESH
            ),
        )

    def t_start(step, carry):
        for copy in t_copies(far_first(step, n_y)):
            copy.start()
        return carry

    lax.fori_loop(0, n_y - 1, t_start, 0, unroll=UNROLL)
    if NEAR_AT == 3:
        near_start()
    t_dst[own_group] = t_src[...]
    tl_dst[own_group] = tl_src[...]

    first = me * rows
    start_column = doc_start_column(doc_ref, first, rows)

    near_pass()

    def t_wait(k, carry):
        slot = (own_group + k) % n_y
        pltpu.make_async_remote_copy(
            t_src, t_dst.at[slot], t_send.at[k], t_recv.at[slot], (me, hx), MESH
        ).wait_recv()
        pltpu.make_async_remote_copy(
            tl_src, tl_dst.at[slot], tl_send.at[k], tl_recv.at[slot], (me, hx), MESH
        ).wait_recv()
        return carry

    lax.fori_loop(1, n_y, t_wait, 0)
    carried = jnp.zeros((width, 128), F32)
    for slot in range(n_y):
        grown = jnp.exp(tl_dst[slot]) * carried + t_dst[slot].astype(F32)
        carried = jnp.where(slot < own_group, grown, carried)
    for slot in range(row):
        onward = jnp.where(core == 1, jnp.exp(la_dst[slot]), 1.0)
        r_src[slot] = (onward * (scan_buf[slot] + jnp.exp(cum_buf[slot]) * carried)).astype(BF16)

    def r_copy(other):
        return pltpu.make_async_remote_copy(
            r_src.at[slot_of(other, row, core)],
            state_ref.at[hx, chip, core],
            r_send.at[other],
            r_recv.at[pos],
            (base + other, hx),
            MESH,
        )

    def r_arrival(other):
        return pltpu.make_async_remote_copy(
            r_src.at[0],
            state_ref.at[hx, other // 2, other % 2],
            r_send.at[other],
            r_recv.at[other],
            (base + other, hx),
            MESH,
        )

    def near_first(step):
        return (chip + n_z + (step + 1) // 2 * (2 * (step % 2) - 1)) % n_z

    def x_copy(part, k):
        return pltpu.make_async_remote_copy(
            state_ref.at[hx, part],
            state_ref.at[hx, part],
            state_send.at[k, part],
            state_recv.at[hx, part],
            (me, (hx + k) % n_head),
            MESH,
        )

    beside = 2 * chip + 1 - core
    r_copy(beside).start()

    def r_start(step, carry):
        for side in (0, 1):
            r_copy(2 * near_first(step) + side).start()
        return carry

    lax.fori_loop(1, n_z, r_start, 0, unroll=UNROLL)
    state_ref[hx, chip, core] = r_src[own_slot]

    r_arrival(beside).wait_recv()
    for k in head_steps:
        x_copy(chip, k).start()

    def r_pass(step, carry):
        part = near_first(step)
        for side in (0, 1):
            r_arrival(2 * part + side).wait_recv()
        for k in head_steps:
            x_copy(part, k).start()
        return carry

    lax.fori_loop(1, n_z, r_pass, 0, unroll=UNROLL)

    for load in loads[4:]:
        load.wait()
    for part in (0, 1):
        far_keys[part].wait_recv()
    columns = rows
    query_pos = (first + iota((rows, columns), 0)).astype(F32)
    start_wide = jnp.broadcast_to(start_column, (rows, columns))
    masks = []
    for distance in range(3):
        key_pos = (first - distance * rows + iota((rows, columns), 1)).astype(F32)
        masks.append((key_pos >= start_wide) & (key_pos <= query_pos))
    lane = iota((rows, 128), 1)
    stats = jnp.where(lane == 4, start_column, 0.0)
    for h in range(2):
        cols = slice(h * HEAD_DIM, (h + 1) * HEAD_DIM)
        query, grad = q_ref[:, cols], do_ref[:, cols]
        keys = [k_ref[:, cols], kv_in[0, 0, :, cols], kv_in[1, 0, :, cols]]
        values = [v_ref[:, cols], kv_in[0, 1, :, cols], kv_in[1, 1, :, cols]]
        scores = [
            jnp.where(mask, dot_nt(query, key) * SCALE, OFF) for mask, key in zip(masks, keys)
        ]
        top = jnp.max(
            jnp.maximum(jnp.maximum(scores[0], scores[1]), scores[2]), axis=1, keepdims=True
        )
        powers = [jnp.exp(score - top) for score in scores]
        total = jnp.sum(powers[0] + powers[1] + powers[2], axis=1, keepdims=True)
        inverse = 1.0 / total
        probs = [power * inverse for power in powers]
        out = sum(dot(prob.astype(BF16), value) for prob, value in zip(probs, values))
        out = out.astype(BF16)
        attn_ref[:, cols] = out
        delta = jnp.sum(grad.astype(F32) * out.astype(F32), axis=1, keepdims=True)
        slopes = [
            (prob * (dot_nt(grad, value) - delta) * SCALE).astype(BF16)
            for prob, value in zip(probs, values)
        ]
        dq_ref[:, cols] = sum(dot(slope, key) for slope, key in zip(slopes, keys)).astype(BF16)
        stats = jnp.where(lane == h, top + jnp.log(total), stats)
        stats = jnp.where(lane == 2 + h, delta, stats)
    stat_out[...] = stats.T[0:8, :]
    stat_copies = [
        pltpu.make_async_remote_copy(
            stat_out,
            stat_in.at[distance - 1],
            stat_send.at[distance - 1],
            stat_recv.at[distance - 1],
            (seq_at(-distance), hx),
            MESH,
        )
        for distance in (1, 2)
    ]
    for copy in stat_copies:
        copy.start()

    def entering(head, side):
        return state_ref[head, :, side].reshape(rows, 128)

    y_ref[...] = (
        carry_weight * (y_inner + dot(c_ref[...], entering(hx, 0)))
        + gain_wide * x_ref[...].astype(F32)
    ).astype(BF16)
    xg_ref[...] = (
        source_weight * (x_inner + dot(b_ref[...], entering(hx, 1)))
        + gain_wide * g_ref[...].astype(F32)
    ).astype(BF16)
    for k in head_steps:
        other = (hx + k) % n_head
        pltpu.make_async_remote_copy(
            mix_ref.at[hx], mix_ref.at[other], mix_send.at[k], mix_recv.at[other], (me, other), MESH
        ).wait_recv()
    anti = iota((rows, rows), 0) <= iota((rows, rows), 1)
    meet = sum(dot_nt(mix_ref[h, 0], mix_ref[h, 1]) for h in range(n_head))
    cg_ref[...] = dot(jnp.where(causal, meet, 0.0).astype(BF16), b_ref[...])
    meet = sum(dot_nt(mix_ref[h, 1], mix_ref[h, 0]) for h in range(n_head))
    bg_ref[...] = dot(jnp.where(anti, meet, 0.0).astype(BF16), c_ref[...])

    key_pos = (first + iota((rows, columns), 0)).astype(F32)
    key_total, value_total = [0.0, 0.0], [0.0, 0.0]
    for distance in range(3):
        if distance == 1:
            for copy in stat_copies:
                copy.wait_recv()
            for part in (0, 1):
                far_queries[part].wait_recv()
        stat = stat_out if distance == 0 else stat_in.at[distance - 1]
        query_pos = (seq_at(distance) * rows + iota((rows, columns), 1)).astype(F32)
        turned = (key_pos >= stat[4:5, :]) & (key_pos <= query_pos)
        for h in range(2):
            cols = slice(h * HEAD_DIM, (h + 1) * HEAD_DIM)
            key, value = k_ref[:, cols], v_ref[:, cols]
            if distance == 0:
                query, grad = q_ref[:, cols], do_ref[:, cols]
            else:
                query, grad = qd_in[distance - 1, 0, :, cols], qd_in[distance - 1, 1, :, cols]
            score = jnp.where(turned, dot_nt(key, query) * SCALE, OFF)
            prob = jnp.exp(score - stat[h : h + 1, :])
            value_total[h] = value_total[h] + dot(prob.astype(BF16), grad)
            slope = prob * (dot_nt(value, grad) - stat[2 + h : 3 + h, :]) * SCALE
            key_total[h] = key_total[h] + dot(slope.astype(BF16), query)
    for h in range(2):
        cols = slice(h * HEAD_DIM, (h + 1) * HEAD_DIM)
        dk_ref[:, cols] = key_total[h].astype(BF16)
        dv_ref[:, cols] = value_total[h].astype(BF16)
    def x_wait(part, carry):
        for k in head_steps:
            other = (hx + k) % n_head
            pltpu.make_async_remote_copy(
                state_ref.at[hx, part],
                state_ref.at[other, part],
                state_send.at[k, part],
                state_recv.at[other, part],
                (me, other),
                MESH,
            ).wait_recv()
        return carry

    lax.fori_loop(0, n_z, x_wait, 0)
    bg_ref[...] += sum(dot_nt(mix_ref[h, 1], entering(h, 1)) for h in range(n_head))
    cg_ref[...] += sum(dot_nt(mix_ref[h, 0], entering(h, 0)) for h in range(n_head))
    for copy in first_copies + mix_copies + stat_copies:
        copy.wait_send()

    @pl.when(core == 0)
    def _():
        for copy in far_keys + pass_keys:
            copy.wait_send()

    @pl.when(core == 1)
    def _():
        for copy in far_queries + pass_queries:
            copy.wait_send()

    def row_sent(k, carry):
        for copy in (*a_copies(k), r_copy((pos + k) % row)):
            copy.wait_send()
        return carry

    lax.fori_loop(1, row, row_sent, 0)

    def group_sent(k, carry):
        for copy in t_copies(k):
            copy.wait_send()
        return carry

    lax.fori_loop(1, n_y, group_sent, 0)

    def x_sent(part, carry):
        for k in head_steps:
            x_copy(part, k).wait_send()
        return carry

    lax.fori_loop(0, n_z, x_sent, 0)


def last_kernel(*refs):
    count = len(refs) // 2
    copies = [
        pltpu.make_async_copy(refs[n], refs[count + n], refs[-1].at[n]) for n in range(count)
    ]
    for copy in copies:
        copy.start()
    for copy in copies:
        copy.wait()


def on_device(
    n_seq,
    n_head,
    n_z,
    queries,
    key_rows,
    value_rows,
    attn_out_grad,
    ssm_input,
    b_matrix,
    c_matrix,
    step_sizes,
    decay_rates,
    skip_gain,
    ssm_out_grad,
    doc_lengths,
):
    rows, columns = queries.shape
    row, n_y, width = 2 * n_z, n_seq // (2 * n_z), rows // n_z
    vmem = pl.BlockSpec(memory_space=pltpu.VMEM)
    smem = pl.BlockSpec(memory_space=pltpu.SMEM)
    hbm = pl.BlockSpec(memory_space=pltpu.HBM)
    states = b_matrix.shape[1]
    shapes = ((rows, columns, BF16),) * 4 + ((rows, 128, BF16),) * 2 + ((rows, states, F32),) * 2
    results = tuple(jax.ShapeDtypeStruct((m, n), kind) for m, n, kind in shapes)
    dma = pltpu.SemaphoreType.DMA
    outs = pl.pallas_call(
        functools.partial(main_kernel, n_seq, n_head, n_z),
        out_shape=results,
        in_specs=[smem, smem] + [vmem] * 2 + [hbm] * 8,
        out_specs=(vmem,) * 8,
        scratch_shapes=[
            pltpu.VMEM((n_head, 2, rows, 128), BF16),
            pltpu.VMEM((n_head, n_z, 2, width, 128), BF16),
            pltpu.VMEM((rows, columns), BF16),
            pltpu.VMEM((rows, columns), BF16),
            pltpu.VMEM((rows, columns), BF16),
            pltpu.VMEM((rows, columns), BF16),
            pltpu.VMEM((rows, 128), BF16),
            pltpu.VMEM((rows, 128), BF16),
            pltpu.VMEM((rows, states), BF16),
            pltpu.VMEM((rows, states), BF16),
            dma((8,)),
            pltpu.VMEM((2, 2, rows, columns), BF16),
            pltpu.VMEM((2, 2, rows, columns), BF16),
            pltpu.VMEM((8, rows), F32),
            pltpu.VMEM((2, 8, rows), F32),
            pltpu.VMEM((row, width, 128), BF16),
            pltpu.VMEM((row, width, 128), BF16),
            pltpu.VMEM((1, 128), F32),
            pltpu.VMEM((row, 1, 128), F32),
            pltpu.VMEM((row, width, 128), F32),
            pltpu.VMEM((row, 1, 128), F32),
            pltpu.VMEM((width, 128), BF16),
            pltpu.VMEM((n_y, width, 128), BF16),
            pltpu.VMEM((1, 128), F32),
            pltpu.VMEM((n_y, 1, 128), F32),
            pltpu.VMEM((row, width, 128), BF16),
            dma((8,)),
            dma((8,)),
            dma((2,)),
            dma((2,)),
            dma((row,)),
            dma((row,)),
            dma((row,)),
            dma((row,)),
            dma((n_y,)),
            dma((n_y,)),
            dma((n_y,)),
            dma((n_y,)),
            dma((row,)),
            dma((row,)),
            dma((n_head,)),
            dma((n_head,)),
            dma((n_head, n_z)),
            dma((n_head, n_z)),
        ],
        compiler_params=pltpu.CompilerParams(
            collective_id=0, has_side_effects=True, vmem_limit_bytes=VMEM_BYTES
        ),
        name="main",
    )(
        decay_rates,
        skip_gain,
        doc_lengths.reshape(1, -1),
        step_sizes.T,
        *[
            pltpu.with_memory_space_constraint(array, pltpu.HBM)
            for array in (
                queries,
                key_rows,
                value_rows,
                attn_out_grad,
                ssm_input,
                ssm_out_grad,
                b_matrix,
                c_matrix,
            )
        ],
    )
    return pl.pallas_call(
        last_kernel,
        out_shape=results,
        in_specs=[vmem] * 8,
        out_specs=(hbm,) * 8,
        scratch_shapes=[dma((8,))],
        compiler_params=pltpu.CompilerParams(vmem_limit_bytes=VMEM_BYTES),
        name="last",
    )(*outs)


def build(mesh, n_z):
    n_seq, n_head = mesh.shape["seq"], mesh.shape["head"]
    tokens = P("seq", "head")
    whole = P("seq", None)
    return jax.shard_map(
        functools.partial(on_device, n_seq, n_head, n_z),
        mesh=mesh,
        in_specs=(
            tokens,
            tokens,
            tokens,
            tokens,
            tokens,
            whole,
            whole,
            tokens,
            P("head"),
            P("head"),
            tokens,
            P(),
        ),
        out_specs=(tokens, tokens, tokens, tokens, tokens, tokens, whole, whole),
        check_vma=False,
    )


def solution(mesh):
    return build(mesh, 8)
```

```python
import functools

import jax
import jax.numpy as jnp
from jax import lax
from jax.experimental import pallas as pl
from jax.experimental.pallas import tpu as pltpu
from jax.sharding import PartitionSpec as P

MESH = pl.DeviceIdType.MESH
HEAD_DIM = 128
SCALE = HEAD_DIM**-0.5
OFF = -1e30
F32 = jnp.float32
BF16 = jnp.bfloat16
UNROLL = True
VMEM_BYTES = 40 * 1024 * 1024


def far_first(step, count):
    odd = step % 2
    return count // 2 + (step // 2 + odd) * (1 - 2 * odd)


def dot(a, b):
    return jnp.dot(a, b, preferred_element_type=F32)


def dot_nt(a, b):
    return lax.dot_general(a, b, (((1,), (1,)), ((), ())), preferred_element_type=F32)


def dot_tn(a, b):
    return lax.dot_general(a, b, (((0,), (0,)), ((), ())), preferred_element_type=F32)


def iota(shape, axis):
    return lax.broadcasted_iota(jnp.int32, shape, axis)


def lower(size):
    return iota((size, size), 1) <= iota((size, size), 0)


def doc_start_column(doc_ref, first, rows):
    docs = doc_ref.shape[1]
    lengths = jnp.broadcast_to(doc_ref[...], (16, docs))
    upper = jnp.where(iota((docs, docs), 0) <= iota((docs, docs), 1), 1.0, 0.0).astype(BF16)
    high, low = lengths // 16, lengths % 16
    ends = 16.0 * dot(high.astype(F32).astype(BF16), upper) + dot(
        low.astype(F32).astype(BF16), upper
    )
    ends = jnp.broadcast_to(ends[0:1, :], (rows, docs))
    position = (first + iota((rows, docs), 0)).astype(F32)
    return jnp.max(jnp.where(ends <= position, ends, 0.0), axis=1, keepdims=True)


def running_sum(rows):
    ones = jnp.where(lower(rows.shape[0]), 1.0, 0.0).astype(BF16)
    high = rows.astype(BF16)
    rest = rows - high.astype(F32)
    middle = rest.astype(BF16)
    low = (rest - middle.astype(F32)).astype(BF16)
    return dot(ones, high) + dot(ones, middle) + dot(ones, low)


def main_kernel(
    n_seq,
    n_head,
    n_z,
    rate_hbm,
    gain_hbm,
    doc_hbm,
    dt_hbm,
    q_hbm,
    k_hbm,
    v_hbm,
    do_hbm,
    x_hbm,
    g_hbm,
    b_hbm,
    c_hbm,
    attn_ref,
    dq_ref,
    dk_ref,
    dv_ref,
    y_ref,
    xg_ref,
    bg_ref,
    cg_ref,
    mix_ref,
    state_ref,
    q_ref,
    k_ref,
    v_ref,
    do_ref,
    x_ref,
    g_ref,
    b_ref,
    c_ref,
    rate_ref,
    gain_ref,
    doc_ref,
    dt_ref,
    load_sem,
    kv_in,
    qd_in,
    stat_out,
    stat_in,
    a_src,
    a_dst,
    la_src,
    la_dst,
    scan_buf,
    cum_buf,
    t_src,
    t_dst,
    tl_src,
    tl_dst,
    r_src,
    near_send,
    near_recv,
    stat_send,
    stat_recv,
    a_send,
    a_recv,
    la_send,
    la_recv,
    t_send,
    t_recv,
    tl_send,
    tl_recv,
    r_send,
    r_recv,
    mix_send,
    mix_recv,
    state_send,
    state_recv,
):
    me = lax.axis_index("seq")
    hx = lax.axis_index("head")
    row = 2 * n_z
    n_y = n_seq // row
    rows = q_ref.shape[0]
    group, pos = me // row, me % row
    chip, core = pos // 2, pos % 2
    base = group * row
    width = rows // n_z

    def seq_at(offset):
        return (me + offset + n_seq) % n_seq

    def wait_all(buffer, count, sem):
        blocks = buffer.at[pl.ds(0, count)]
        pltpu.make_async_copy(blocks, blocks, sem).wait()

    def slot_of(index, count, side):
        return index + side * (count - 1 - 2 * index)

    loads = [
        pltpu.make_async_copy(source, target, load_sem.at[at])
        for at, (source, target) in enumerate(
            (
                (dt_hbm, dt_ref),
                (rate_hbm, rate_ref),
                (gain_hbm, gain_ref),
                (x_hbm, x_ref),
                (b_hbm, b_ref),
                (g_hbm, g_ref),
                (c_hbm, c_ref),
                (q_hbm, q_ref),
                (k_hbm, k_ref),
                (v_hbm, v_ref),
                (do_hbm, do_ref),
                (doc_hbm, doc_ref),
            )
        )
    ]
    for load in loads:
        load.start()

    barrier = pltpu.get_barrier_semaphore()

    def greet(seq_index, head_index):
        pl.semaphore_signal(
            barrier, inc=1, device_id=(seq_index, head_index), device_id_type=MESH
        )

    for offset in (-2, -1, 1, 2):
        greet(seq_at(offset), hx)

    def greet_row(k, carry):
        greet(base + (pos + k) % row, hx)
        return carry

    lax.fori_loop(1, row, greet_row, 0)

    def greet_group(k, carry):
        greet(((group + k) % n_y) * row + pos, hx)
        return carry

    lax.fori_loop(1, n_y, greet_group, 0)
    for k in range(1, n_head):
        greet(me, (hx + k) % n_head)

    for load in loads[:3]:
        load.wait()
    lanes_low = iota((rows, 128), 1) < 64
    dt_wide = jnp.concatenate(
        [
            jnp.broadcast_to(dt_ref[0:1, :], (64, rows)),
            jnp.broadcast_to(dt_ref[1:2, :], (64, rows)),
        ],
        axis=0,
    ).T
    rate_wide = jnp.where(lanes_low, rate_ref[0], rate_ref[1])
    gain_wide = jnp.where(lanes_low, gain_ref[0], gain_ref[1])
    log_decay = running_sum(-dt_wide * rate_wide)
    carry_weight = jnp.exp(log_decay)
    source_weight = jnp.exp(-log_decay) * dt_wide
    last = log_decay[rows - 1 : rows, :]
    decay_all = jnp.exp(last)
    for load in loads[3:7]:
        load.wait()
    mix_ref[hx, 0] = (carry_weight * g_ref[...].astype(F32)).astype(BF16)
    mix_ref[hx, 1] = (source_weight * x_ref[...].astype(F32)).astype(BF16)
    local_state = (decay_all * dot_tn(b_ref[...], mix_ref[hx, 1])).astype(BF16)
    local_adjoint = dot_tn(c_ref[...], mix_ref[hx, 0]).astype(BF16)
    for z in range(n_z):
        a_src[2 * z] = local_state[z * width : (z + 1) * width, :]
        a_src[2 * z + 1] = local_adjoint[z * width : (z + 1) * width, :]
    la_src[...] = last

    pl.semaphore_wait(barrier, 4 + (row - 1) + (n_y - 1) + (n_head - 1))

    def a_copies(k):
        owner = (pos + k) % row
        slot = slot_of(pos, row, owner % 2)
        target = (base + owner, hx)
        return (
            pltpu.make_async_remote_copy(
                a_src.at[owner], a_dst.at[slot], a_send.at[0], a_recv.at[0], target, MESH
            ),
            pltpu.make_async_remote_copy(
                la_src, la_dst.at[slot], la_send.at[0], la_recv.at[0], target, MESH
            ),
        )

    def a_start(step, carry):
        for copy in a_copies(far_first(step, row)):
            copy.start()
        return carry

    lax.fori_loop(0, row - 1, a_start, 0, unroll=UNROLL)
    own_slot = slot_of(pos, row, core)
    a_dst[own_slot] = a_src[pos]
    la_dst[own_slot] = la_src[...]

    def near_copy(source, place, part, at, offset, sem):
        return pltpu.make_async_remote_copy(
            source,
            place.at[at, part],
            near_send.at[sem],
            near_recv.at[(2 if place is qd_in else 0) + 4 * at + part],
            (seq_at(offset), hx),
            MESH,
        )

    keys_hbm, queries_hbm = (k_hbm, v_hbm), (q_hbm, do_hbm)
    first_copies = [near_copy(keys_hbm[p], kv_in, p, 0, 1, p) for p in (0, 1)]
    first_copies += [near_copy(queries_hbm[p], qd_in, p, 0, -1, 2 + p) for p in (0, 1)]
    far_keys = [near_copy(keys_hbm[p], kv_in, p, 1, 2, 4 + p) for p in (0, 1)]
    far_queries = [near_copy(queries_hbm[p], qd_in, p, 1, -2, 4 + p) for p in (0, 1)]
    pass_keys = [near_copy(kv_in.at[0, p], kv_in, p, 1, 1, 6 + p) for p in (0, 1)]
    pass_queries = [near_copy(qd_in.at[0, p], qd_in, p, 1, -1, 6 + p) for p in (0, 1)]

    def near_start():
        for copy in first_copies:
            copy.start()

        @pl.when(core == 0)
        def _():
            for copy in far_keys:
                copy.start()

        @pl.when(core == 1)
        def _():
            for copy in far_queries:
                copy.start()

    def relay(arriving, onward):
        for copy, passed in zip(arriving, onward):
            copy.wait_recv()
            passed.start()

    def mix_copy(k):
        return pltpu.make_async_remote_copy(
            mix_ref.at[hx],
            mix_ref.at[hx],
            mix_send.at[k],
            mix_recv.at[hx],
            (me, (hx + k) % n_head),
            MESH,
        )

    head_steps = [far_first(step, n_head) for step in range(n_head - 1)]
    mix_copies = [mix_copy(k) for k in head_steps]
    for copy in mix_copies:
        copy.start()

    causal = lower(rows)
    meet = jnp.where(causal, dot_nt(c_ref[...], b_ref[...]), 0.0).astype(BF16)
    y_inner = dot(meet, mix_ref[hx, 1])
    meet_back = jnp.where(
        iota((rows, rows), 0) <= iota((rows, rows), 1), dot_nt(b_ref[...], c_ref[...]), 0.0
    ).astype(BF16)
    x_inner = dot(meet_back, mix_ref[hx, 0])

    wait_all(a_dst, row - 1, a_recv.at[0])
    wait_all(la_dst, row - 1, la_recv.at[0])

    state = jnp.zeros((width, 128), F32)
    summed = jnp.zeros((1, 128), F32)
    for slot in range(row):
        scan_buf[slot] = state
        cum_buf[slot] = summed
        state = jnp.exp(la_dst[slot]) * state + a_dst[slot].astype(F32)
        summed = summed + la_dst[slot]
    t_src[...] = state.astype(BF16)
    tl_src[...] = summed

    own_group = slot_of(group, n_y, core)

    def t_copies(k):
        target = (((group + k) % n_y) * row + pos, hx)
        return (
            pltpu.make_async_remote_copy(
                t_src, t_dst.at[own_group], t_send.at[0], t_recv.at[0], target, MESH
            ),
            pltpu.make_async_remote_copy(
                tl_src, tl_dst.at[own_group], tl_send.at[0], tl_recv.at[0], target, MESH
            ),
        )

    def t_start(step, carry):
        for copy in t_copies(far_first(step, n_y)):
            copy.start()
        return carry

    lax.fori_loop(0, n_y - 1, t_start, 0, unroll=UNROLL)
    near_start()
    t_dst[own_group] = t_src[...]
    tl_dst[own_group] = tl_src[...]

    first = me * rows
    loads[11].wait()
    start_column = doc_start_column(doc_ref, first, rows)

    columns = rows
    stat_copies = [
        pltpu.make_async_remote_copy(
            stat_out,
            stat_in.at[distance - 1],
            stat_send.at[distance - 1],
            stat_recv.at[distance - 1],
            (seq_at(-distance), hx),
            MESH,
        )
        for distance in (1, 2)
    ]

    def forward():
        for load in loads[7:11]:
            load.wait()
        @pl.when(core == 1)
        def _():
            for copy in first_copies[:2]:
                copy.wait_recv()

        for part in (0, 1):
            far_keys[part].wait_recv()
        query_pos = (first + iota((rows, columns), 0)).astype(F32)
        start_wide = jnp.broadcast_to(start_column, (rows, columns))
        masks = []
        for distance in range(3):
            key_pos = (first - distance * rows + iota((rows, columns), 1)).astype(F32)
            masks.append((key_pos >= start_wide) & (key_pos <= query_pos))
        lane = iota((rows, 128), 1)
        stats = jnp.where(lane == 4, start_column, 0.0)
        for h in range(2):
            cols = slice(h * HEAD_DIM, (h + 1) * HEAD_DIM)
            query, grad = q_ref[:, cols], do_ref[:, cols]
            keys = [k_ref[:, cols], kv_in[0, 0, :, cols], kv_in[1, 0, :, cols]]
            values = [v_ref[:, cols], kv_in[0, 1, :, cols], kv_in[1, 1, :, cols]]
            scores = [
                jnp.where(mask, dot_nt(query, key) * SCALE, OFF) for mask, key in zip(masks, keys)
            ]
            top = jnp.max(
                jnp.maximum(jnp.maximum(scores[0], scores[1]), scores[2]), axis=1, keepdims=True
            )
            powers = [jnp.exp(score - top) for score in scores]
            total = jnp.sum(powers[0] + powers[1] + powers[2], axis=1, keepdims=True)
            inverse = 1.0 / total
            probs = [power * inverse for power in powers]
            out = sum(dot(prob.astype(BF16), value) for prob, value in zip(probs, values))
            out = out.astype(BF16)
            attn_ref[:, cols] = out
            delta = jnp.sum(grad.astype(F32) * out.astype(F32), axis=1, keepdims=True)
            slopes = [
                (prob * (dot_nt(grad, value) - delta) * SCALE).astype(BF16)
                for prob, value in zip(probs, values)
            ]
            dq_ref[:, cols] = sum(dot(slope, key) for slope, key in zip(slopes, keys)).astype(BF16)
            stats = jnp.where(lane == h, top + jnp.log(total), stats)
            stats = jnp.where(lane == 2 + h, delta, stats)
        stat_out[...] = stats.T[0:8, :]
        for copy in stat_copies:
            copy.start()

    def inner():
        for k in head_steps:
            other = (hx + k) % n_head
            pltpu.make_async_remote_copy(
                mix_ref.at[hx], mix_ref.at[other], mix_send.at[k], mix_recv.at[other], (me, other), MESH
            ).wait_recv()
        anti = iota((rows, rows), 0) <= iota((rows, rows), 1)
        meet = sum(dot_nt(mix_ref[h, 0], mix_ref[h, 1]) for h in range(n_head))
        cg_ref[...] = dot(jnp.where(causal, meet, 0.0).astype(BF16), b_ref[...])
        meet = sum(dot_nt(mix_ref[h, 1], mix_ref[h, 0]) for h in range(n_head))
        bg_ref[...] = dot(jnp.where(anti, meet, 0.0).astype(BF16), c_ref[...])

    def backward():
        key_pos = (first + iota((rows, columns), 0)).astype(F32)
        key_total, value_total = [0.0, 0.0], [0.0, 0.0]
        for distance in range(3):
            if distance == 1:
                for copy in stat_copies:
                    copy.wait_recv()


                @pl.when(core == 0)
                def _():
                    for copy in first_copies[2:]:
                        copy.wait_recv()

                for part in (0, 1):
                    far_queries[part].wait_recv()
            stat = stat_out if distance == 0 else stat_in.at[distance - 1]
            query_pos = (seq_at(distance) * rows + iota((rows, columns), 1)).astype(F32)
            turned = (key_pos >= stat[4:5, :]) & (key_pos <= query_pos)
            for h in range(2):
                cols = slice(h * HEAD_DIM, (h + 1) * HEAD_DIM)
                key, value = k_ref[:, cols], v_ref[:, cols]
                if distance == 0:
                    query, grad = q_ref[:, cols], do_ref[:, cols]
                else:
                    query, grad = qd_in[distance - 1, 0, :, cols], qd_in[distance - 1, 1, :, cols]
                score = jnp.where(turned, dot_nt(key, query) * SCALE, OFF)
                prob = jnp.exp(score - stat[h : h + 1, :])
                value_total[h] = value_total[h] + dot(prob.astype(BF16), grad)
                slope = prob * (dot_nt(value, grad) - stat[2 + h : 3 + h, :]) * SCALE
                key_total[h] = key_total[h] + dot(slope.astype(BF16), query)
        for h in range(2):
            cols = slice(h * HEAD_DIM, (h + 1) * HEAD_DIM)
            dk_ref[:, cols] = key_total[h].astype(BF16)
            dv_ref[:, cols] = value_total[h].astype(BF16)


    wait_all(t_dst, n_y - 1, t_recv.at[0])
    wait_all(tl_dst, n_y - 1, tl_recv.at[0])
    carried = jnp.zeros((width, 128), F32)
    for slot in range(n_y):
        grown = jnp.exp(tl_dst[slot]) * carried + t_dst[slot].astype(F32)
        carried = jnp.where(slot < own_group, grown, carried)
    for slot in range(row):
        onward = jnp.where(core == 1, jnp.exp(la_dst[slot]), 1.0)
        r_src[slot] = (onward * (scan_buf[slot] + jnp.exp(cum_buf[slot]) * carried)).astype(BF16)

    def r_copy(other):
        return pltpu.make_async_remote_copy(
            r_src.at[slot_of(other, row, core)],
            state_ref.at[hx, chip, core],
            r_send.at[0],
            r_recv.at[pos],
            (base + other, hx),
            MESH,
        )

    def r_arrival(other):
        return pltpu.make_async_remote_copy(
            r_src.at[0],
            state_ref.at[hx, other // 2, other % 2],
            r_send.at[0],
            r_recv.at[other],
            (base + other, hx),
            MESH,
        )

    def near_first(step):
        return (chip + n_z + (step + 1) // 2 * (2 * (step % 2) - 1)) % n_z

    def x_copy(part, k):
        return pltpu.make_async_remote_copy(
            state_ref.at[hx, part],
            state_ref.at[hx, part],
            state_send.at[k],
            state_recv.at[hx],
            (me, (hx + k) % n_head),
            MESH,
        )

    beside = 2 * chip + 1 - core
    r_copy(beside).start()

    def r_start(step, carry):
        for side in (0, 1):
            r_copy(2 * near_first(step) + side).start()
        return carry

    lax.fori_loop(1, n_z, r_start, 0, unroll=UNROLL)
    state_ref[hx, chip, core] = r_src[own_slot]

    r_arrival(beside).wait_recv()
    for k in head_steps:
        x_copy(chip, k).start()

    def r_pass(step, carry):
        part = near_first(step)
        for side in (0, 1):
            r_arrival(2 * part + side).wait_recv()
        for k in head_steps:
            x_copy(part, k).start()
        return carry

    lax.fori_loop(1, n_z, r_pass, 0, unroll=UNROLL)

    pl.when(core == 0)(lambda: relay(first_copies[:2], pass_keys))
    pl.when(core == 1)(lambda: relay(first_copies[2:], pass_queries))
    forward()
    def entering(head, side):
        return state_ref[head, :, side].reshape(rows, 128)

    y_ref[...] = (
        carry_weight * (y_inner + dot(c_ref[...], entering(hx, 0)))
        + gain_wide * x_ref[...].astype(F32)
    ).astype(BF16)
    xg_ref[...] = (
        source_weight * (x_inner + dot(b_ref[...], entering(hx, 1)))
        + gain_wide * g_ref[...].astype(F32)
    ).astype(BF16)
    inner()
    backward()

    for copy in first_copies + mix_copies + stat_copies:
        copy.wait_send()

    @pl.when(core == 0)
    def _():
        for copy in far_keys + pass_keys:
            copy.wait_send()

    @pl.when(core == 1)
    def _():
        for copy in far_queries + pass_queries:
            copy.wait_send()

    wait_all(a_src, row - 1, a_send.at[0])
    wait_all(la_dst, row - 1, la_send.at[0])
    wait_all(t_dst, n_y - 1, t_send.at[0])
    wait_all(tl_dst, n_y - 1, tl_send.at[0])
    wait_all(r_src, row - 1, r_send.at[0])

    for k in head_steps:
        wait_all(state_ref.at[hx], n_z, state_send.at[k])
    for k in head_steps:
        other = (hx + k) % n_head
        wait_all(state_ref.at[other], n_z, state_recv.at[other])
    bg_ref[...] += sum(dot_nt(mix_ref[h, 1], entering(h, 1)) for h in range(n_head))
    cg_ref[...] += sum(dot_nt(mix_ref[h, 0], entering(h, 0)) for h in range(n_head))


def last_kernel(*refs):
    count = len(refs) // 2
    copies = [
        pltpu.make_async_copy(refs[n], refs[count + n], refs[-1].at[n]) for n in range(count)
    ]
    for copy in copies:
        copy.start()
    for copy in copies:
        copy.wait()


def on_device(
    n_seq,
    n_head,
    n_z,
    queries,
    key_rows,
    value_rows,
    attn_out_grad,
    ssm_input,
    b_matrix,
    c_matrix,
    step_sizes,
    decay_rates,
    skip_gain,
    ssm_out_grad,
    doc_lengths,
):
    rows, columns = queries.shape
    row, n_y, width = 2 * n_z, n_seq // (2 * n_z), rows // n_z
    vmem = pl.BlockSpec(memory_space=pltpu.VMEM)
    hbm = pl.BlockSpec(memory_space=pltpu.HBM)
    states = b_matrix.shape[1]
    shapes = ((rows, columns, BF16),) * 4 + ((rows, 128, BF16),) * 2 + ((rows, states, F32),) * 2
    results = tuple(jax.ShapeDtypeStruct((m, n), kind) for m, n, kind in shapes)
    dma = pltpu.SemaphoreType.DMA
    outs = pl.pallas_call(
        functools.partial(main_kernel, n_seq, n_head, n_z),
        out_shape=results,
        in_specs=[hbm] * 12,
        out_specs=(vmem,) * 8,
        scratch_shapes=[
            pltpu.VMEM((n_head, 2, rows, 128), BF16),
            pltpu.VMEM((n_head, n_z, 2, width, 128), BF16),
            pltpu.VMEM((rows, columns), BF16),
            pltpu.VMEM((rows, columns), BF16),
            pltpu.VMEM((rows, columns), BF16),
            pltpu.VMEM((rows, columns), BF16),
            pltpu.VMEM((rows, 128), BF16),
            pltpu.VMEM((rows, 128), BF16),
            pltpu.VMEM((rows, states), BF16),
            pltpu.VMEM((rows, states), BF16),
            pltpu.SMEM(decay_rates.shape, F32),
            pltpu.SMEM(skip_gain.shape, F32),
            pltpu.VMEM((1, doc_lengths.shape[0]), jnp.int32),
            pltpu.VMEM((step_sizes.shape[1], rows), F32),
            dma((12,)),
            pltpu.VMEM((2, 2, rows, columns), BF16),
            pltpu.VMEM((2, 2, rows, columns), BF16),
            pltpu.VMEM((8, rows), F32),
            pltpu.VMEM((2, 8, rows), F32),
            pltpu.VMEM((row, width, 128), BF16),
            pltpu.VMEM((row, width, 128), BF16),
            pltpu.VMEM((1, 128), F32),
            pltpu.VMEM((row, 1, 128), F32),
            pltpu.VMEM((row, width, 128), F32),
            pltpu.VMEM((row, 1, 128), F32),
            pltpu.VMEM((width, 128), BF16),
            pltpu.VMEM((n_y, width, 128), BF16),
            pltpu.VMEM((1, 128), F32),
            pltpu.VMEM((n_y, 1, 128), F32),
            pltpu.VMEM((row, width, 128), BF16),
            dma((8,)),
            dma((8,)),
            dma((2,)),
            dma((2,)),
            *[dma((1,))] * 9,
            dma((row,)),
            dma((n_head,)),
            dma((n_head,)),
            dma((n_head,)),
            dma((n_head,)),
        ],
        compiler_params=pltpu.CompilerParams(
            collective_id=0, has_side_effects=True, vmem_limit_bytes=VMEM_BYTES
        ),
        name="main",
    )(
        *[
            pltpu.with_memory_space_constraint(array, pltpu.HBM)
            for array in (
                decay_rates,
                skip_gain,
                doc_lengths.reshape(1, -1),
                step_sizes.T,
                queries,
                key_rows,
                value_rows,
                attn_out_grad,
                ssm_input,
                ssm_out_grad,
                b_matrix,
                c_matrix,
            )
        ],
    )
    return pl.pallas_call(
        last_kernel,
        out_shape=results,
        in_specs=[vmem] * 8,
        out_specs=(hbm,) * 8,
        scratch_shapes=[dma((8,))],
        compiler_params=pltpu.CompilerParams(vmem_limit_bytes=VMEM_BYTES),
        name="last",
    )(*outs)


def build(mesh, n_z):
    n_seq, n_head = mesh.shape["seq"], mesh.shape["head"]
    tokens = P("seq", "head")
    whole = P("seq", None)
    return jax.shard_map(
        functools.partial(on_device, n_seq, n_head, n_z),
        mesh=mesh,
        in_specs=(
            tokens,
            tokens,
            tokens,
            tokens,
            tokens,
            whole,
            whole,
            tokens,
            P("head"),
            P("head"),
            tokens,
            P(),
        ),
        out_specs=(tokens, tokens, tokens, tokens, tokens, tokens, whole, whole),
        check_vma=False,
    )


def solution(mesh):
    return build(mesh, 8)
```

```python
import functools

import jax
import jax.numpy as jnp
from jax import lax
from jax.experimental import pallas as pl
from jax.experimental.pallas import tpu as pltpu
from jax.sharding import PartitionSpec as P

MESH = pl.DeviceIdType.MESH
HEAD_DIM = 128
SCALE = HEAD_DIM**-0.5
OFF = -1e30
F32 = jnp.float32
BF16 = jnp.bfloat16
UNROLL = True
VMEM_BYTES = 40 * 1024 * 1024


def far_first(step, count):
    odd = step % 2
    return count // 2 + (step // 2 + odd) * (1 - 2 * odd)


def dot(a, b):
    return jnp.dot(a, b, preferred_element_type=F32)


def dot_nt(a, b):
    return lax.dot_general(a, b, (((1,), (1,)), ((), ())), preferred_element_type=F32)


def dot_tn(a, b):
    return lax.dot_general(a, b, (((0,), (0,)), ((), ())), preferred_element_type=F32)


def iota(shape, axis):
    return lax.broadcasted_iota(jnp.int32, shape, axis)


def lower(size):
    return iota((size, size), 1) <= iota((size, size), 0)


def doc_start_column(doc_ref, first, rows):
    docs = doc_ref.shape[1]
    lengths = jnp.broadcast_to(doc_ref[...], (16, docs))
    upper = jnp.where(iota((docs, docs), 0) <= iota((docs, docs), 1), 1.0, 0.0).astype(BF16)
    high, low = lengths // 16, lengths % 16
    ends = 16.0 * dot(high.astype(F32).astype(BF16), upper) + dot(
        low.astype(F32).astype(BF16), upper
    )
    ends = jnp.broadcast_to(ends[0:1, :], (rows, docs))
    position = (first + iota((rows, docs), 0)).astype(F32)
    return jnp.max(jnp.where(ends <= position, ends, 0.0), axis=1, keepdims=True)


def running_sum(rows):
    ones = jnp.where(lower(rows.shape[0]), 1.0, 0.0).astype(BF16)
    high = rows.astype(BF16)
    rest = rows - high.astype(F32)
    middle = rest.astype(BF16)
    low = (rest - middle.astype(F32)).astype(BF16)
    return dot(ones, high) + dot(ones, middle) + dot(ones, low)


def main_kernel(
    n_seq,
    n_head,
    n_z,
    rate_hbm,
    gain_hbm,
    doc_hbm,
    dt_hbm,
    q_hbm,
    k_hbm,
    v_hbm,
    do_hbm,
    x_hbm,
    g_hbm,
    b_hbm,
    c_hbm,
    attn_ref,
    dq_ref,
    dk_ref,
    dv_ref,
    y_ref,
    xg_ref,
    bg_ref,
    cg_ref,
    mix_ref,
    state_ref,
    q_ref,
    k_ref,
    v_ref,
    do_ref,
    x_ref,
    g_ref,
    b_ref,
    c_ref,
    rate_ref,
    gain_ref,
    doc_ref,
    dt_ref,
    load_sem,
    kv_in,
    qd_in,
    stat_out,
    stat_in,
    a_src,
    a_dst,
    la_src,
    la_dst,
    scan_buf,
    cum_buf,
    t_src,
    t_dst,
    tl_src,
    tl_dst,
    r_src,
    near_send,
    near_recv,
    stat_send,
    stat_recv,
    a_send,
    a_recv,
    la_send,
    la_recv,
    t_send,
    t_recv,
    tl_send,
    tl_recv,
    r_send,
    r_recv,
    mix_send,
    mix_recv,
    state_send,
    state_recv,
):
    me = lax.axis_index("seq")
    hx = lax.axis_index("head")
    row = 2 * n_z
    n_y = n_seq // row
    rows = q_ref.shape[0]
    group, pos = me // row, me % row
    chip, core = pos // 2, pos % 2
    base = group * row
    width = rows // n_z

    def seq_at(offset):
        return (me + offset + n_seq) % n_seq

    def wait_all(buffer, count, sem):
        blocks = buffer.at[pl.ds(0, count)]
        pltpu.make_async_copy(blocks, blocks, sem).wait()

    def slot_of(index, count, side):
        return index + side * (count - 1 - 2 * index)

    loads = [
        pltpu.make_async_copy(source, target, load_sem.at[at])
        for at, (source, target) in enumerate(
            (
                (dt_hbm, dt_ref),
                (rate_hbm, rate_ref),
                (gain_hbm, gain_ref),
                (x_hbm, x_ref),
                (b_hbm, b_ref),
                (g_hbm, g_ref),
                (c_hbm, c_ref),
                (q_hbm, q_ref),
                (k_hbm, k_ref),
                (v_hbm, v_ref),
                (do_hbm, do_ref),
                (doc_hbm, doc_ref),
            )
        )
    ]
    for load in loads:
        load.start()

    barrier = pltpu.get_barrier_semaphore()

    def greet(seq_index, head_index):
        pl.semaphore_signal(
            barrier, inc=1, device_id=(seq_index, head_index), device_id_type=MESH
        )

    for offset in (-2, -1, 1, 2):
        greet(seq_at(offset), hx)

    def greet_row(k, carry):
        greet(base + (pos + k) % row, hx)
        return carry

    lax.fori_loop(1, row, greet_row, 0, unroll=True)

    def greet_group(k, carry):
        greet(((group + k) % n_y) * row + pos, hx)
        return carry

    lax.fori_loop(1, n_y, greet_group, 0, unroll=True)
    for k in range(1, n_head):
        greet(me, (hx + k) % n_head)

    for load in loads[:3]:
        load.wait()
    lanes_low = iota((rows, 128), 1) < 64
    dt_wide = jnp.concatenate(
        [
            jnp.broadcast_to(dt_ref[0:1, :], (64, rows)),
            jnp.broadcast_to(dt_ref[1:2, :], (64, rows)),
        ],
        axis=0,
    ).T
    rate_wide = jnp.where(lanes_low, rate_ref[0], rate_ref[1])
    gain_wide = jnp.where(lanes_low, gain_ref[0], gain_ref[1])
    log_decay = running_sum(-dt_wide * rate_wide)
    carry_weight = jnp.exp(log_decay)
    source_weight = jnp.exp(-log_decay) * dt_wide
    last = log_decay[rows - 1 : rows, :]
    decay_all = jnp.exp(last)
    for load in loads[3:7]:
        load.wait()
    mix_ref[hx, 0] = (carry_weight * g_ref[...].astype(F32)).astype(BF16)
    mix_ref[hx, 1] = (source_weight * x_ref[...].astype(F32)).astype(BF16)
    local_state = (decay_all * dot_tn(b_ref[...], mix_ref[hx, 1])).astype(BF16)
    local_adjoint = dot_tn(c_ref[...], mix_ref[hx, 0]).astype(BF16)
    for z in range(n_z):
        a_src[2 * z] = local_state[z * width : (z + 1) * width, :]
        a_src[2 * z + 1] = local_adjoint[z * width : (z + 1) * width, :]
    la_src[...] = last

    pl.semaphore_wait(barrier, 4 + (row - 1) + (n_y - 1) + (n_head - 1))

    def a_copies(k):
        owner = (pos + k) % row
        slot = slot_of(pos, row, owner % 2)
        target = (base + owner, hx)
        return (
            pltpu.make_async_remote_copy(
                a_src.at[owner], a_dst.at[slot], a_send.at[0], a_recv.at[0], target, MESH
            ),
            pltpu.make_async_remote_copy(
                la_src, la_dst.at[slot], la_send.at[0], la_recv.at[0], target, MESH
            ),
        )

    def a_start(step, carry):
        for copy in a_copies(far_first(step, row)):
            copy.start()
        return carry

    lax.fori_loop(0, row - 1, a_start, 0, unroll=UNROLL)
    own_slot = slot_of(pos, row, core)
    a_dst[own_slot] = a_src[pos]
    la_dst[own_slot] = la_src[...]

    def near_copy(source, place, part, at, offset, sem):
        return pltpu.make_async_remote_copy(
            source,
            place.at[at, part],
            near_send.at[sem],
            near_recv.at[(2 if place is qd_in else 0) + 4 * at + part],
            (seq_at(offset), hx),
            MESH,
        )

    keys_hbm, queries_hbm = (k_hbm, v_hbm), (q_hbm, do_hbm)
    first_copies = [near_copy(keys_hbm[p], kv_in, p, 0, 1, p) for p in (0, 1)]
    first_copies += [near_copy(queries_hbm[p], qd_in, p, 0, -1, 2 + p) for p in (0, 1)]
    far_keys = [near_copy(keys_hbm[p], kv_in, p, 1, 2, 4 + p) for p in (0, 1)]
    far_queries = [near_copy(queries_hbm[p], qd_in, p, 1, -2, 4 + p) for p in (0, 1)]
    pass_keys = [near_copy(kv_in.at[0, p], kv_in, p, 1, 1, 6 + p) for p in (0, 1)]
    pass_queries = [near_copy(qd_in.at[0, p], qd_in, p, 1, -1, 6 + p) for p in (0, 1)]

    def near_start():
        for copy in first_copies:
            copy.start()

        @pl.when(core == 0)
        def _():
            for copy in far_keys:
                copy.start()

        @pl.when(core == 1)
        def _():
            for copy in far_queries:
                copy.start()

    def relay(arriving, onward):
        for copy, passed in zip(arriving, onward):
            copy.wait_recv()
            passed.start()

    def mix_copy(k):
        return pltpu.make_async_remote_copy(
            mix_ref.at[hx],
            mix_ref.at[hx],
            mix_send.at[k],
            mix_recv.at[hx],
            (me, (hx + k) % n_head),
            MESH,
        )

    head_steps = [far_first(step, n_head) for step in range(n_head - 1)]
    mix_copies = [mix_copy(k) for k in head_steps]
    causal = lower(rows)
    meet = jnp.where(causal, dot_nt(c_ref[...], b_ref[...]), 0.0).astype(BF16)
    y_inner = dot(meet, mix_ref[hx, 1])
    meet_back = jnp.where(
        iota((rows, rows), 0) <= iota((rows, rows), 1), dot_nt(b_ref[...], c_ref[...]), 0.0
    ).astype(BF16)
    x_inner = dot(meet_back, mix_ref[hx, 0])

    wait_all(a_dst, row - 1, a_recv.at[0])
    wait_all(la_dst, row - 1, la_recv.at[0])

    state = jnp.zeros((width, 128), F32)
    summed = jnp.zeros((1, 128), F32)
    for slot in range(row):
        scan_buf[slot] = state
        cum_buf[slot] = summed
        state = jnp.exp(la_dst[slot]) * state + a_dst[slot].astype(F32)
        summed = summed + la_dst[slot]
    t_src[...] = state.astype(BF16)
    tl_src[...] = summed

    own_group = slot_of(group, n_y, core)

    def t_copies(k):
        target = (((group + k) % n_y) * row + pos, hx)
        return (
            pltpu.make_async_remote_copy(
                t_src, t_dst.at[own_group], t_send.at[0], t_recv.at[0], target, MESH
            ),
            pltpu.make_async_remote_copy(
                tl_src, tl_dst.at[own_group], tl_send.at[0], tl_recv.at[0], target, MESH
            ),
        )

    def t_start(step, carry):
        for copy in t_copies(far_first(step, n_y)):
            copy.start()
        return carry

    lax.fori_loop(0, n_y - 1, t_start, 0, unroll=UNROLL)
    near_start()
    for copy in mix_copies:
        copy.start()
    t_dst[own_group] = t_src[...]
    tl_dst[own_group] = tl_src[...]

    first = me * rows
    loads[11].wait()
    start_column = doc_start_column(doc_ref, first, rows)

    columns = rows
    stat_copies = [
        pltpu.make_async_remote_copy(
            stat_out,
            stat_in.at[distance - 1],
            stat_send.at[distance - 1],
            stat_recv.at[distance - 1],
            (seq_at(-distance), hx),
            MESH,
        )
        for distance in (1, 2)
    ]

    def forward():
        for load in loads[7:11]:
            load.wait()
        @pl.when(core == 1)
        def _():
            for copy in first_copies[:2]:
                copy.wait_recv()

        for part in (0, 1):
            far_keys[part].wait_recv()
        query_pos = (first + iota((rows, columns), 0)).astype(F32)
        start_wide = jnp.broadcast_to(start_column, (rows, columns))
        masks = []
        for distance in range(3):
            key_pos = (first - distance * rows + iota((rows, columns), 1)).astype(F32)
            masks.append((key_pos >= start_wide) & (key_pos <= query_pos))
        lane = iota((rows, 128), 1)
        stats = jnp.where(lane == 4, start_column, 0.0)
        for h in range(2):
            cols = slice(h * HEAD_DIM, (h + 1) * HEAD_DIM)
            query, grad = q_ref[:, cols], do_ref[:, cols]
            keys = [k_ref[:, cols], kv_in[0, 0, :, cols], kv_in[1, 0, :, cols]]
            values = [v_ref[:, cols], kv_in[0, 1, :, cols], kv_in[1, 1, :, cols]]
            scores = [
                jnp.where(mask, dot_nt(query, key) * SCALE, OFF) for mask, key in zip(masks, keys)
            ]
            top = jnp.max(
                jnp.maximum(jnp.maximum(scores[0], scores[1]), scores[2]), axis=1, keepdims=True
            )
            powers = [jnp.exp(score - top) for score in scores]
            total = jnp.sum(powers[0] + powers[1] + powers[2], axis=1, keepdims=True)
            inverse = 1.0 / total
            probs = [power * inverse for power in powers]
            out = sum(dot(prob.astype(BF16), value) for prob, value in zip(probs, values))
            out = out.astype(BF16)
            attn_ref[:, cols] = out
            delta = jnp.sum(grad.astype(F32) * out.astype(F32), axis=1, keepdims=True)
            slopes = [
                (prob * (dot_nt(grad, value) - delta) * SCALE).astype(BF16)
                for prob, value in zip(probs, values)
            ]
            dq_ref[:, cols] = sum(dot(slope, key) for slope, key in zip(slopes, keys)).astype(BF16)
            stats = jnp.where(lane == h, top + jnp.log(total), stats)
            stats = jnp.where(lane == 2 + h, delta, stats)
        stat_out[...] = stats.T[0:8, :]
        for copy in stat_copies:
            copy.start()

    def inner():
        for k in head_steps:
            other = (hx + k) % n_head
            pltpu.make_async_remote_copy(
                mix_ref.at[hx], mix_ref.at[other], mix_send.at[k], mix_recv.at[other], (me, other), MESH
            ).wait_recv()
        anti = iota((rows, rows), 0) <= iota((rows, rows), 1)
        meet = sum(dot_nt(mix_ref[h, 0], mix_ref[h, 1]) for h in range(n_head))
        cg_ref[...] = dot(jnp.where(causal, meet, 0.0).astype(BF16), b_ref[...])
        meet = sum(dot_nt(mix_ref[h, 1], mix_ref[h, 0]) for h in range(n_head))
        bg_ref[...] = dot(jnp.where(anti, meet, 0.0).astype(BF16), c_ref[...])

    def backward():
        key_pos = (first + iota((rows, columns), 0)).astype(F32)
        key_total, value_total = [0.0, 0.0], [0.0, 0.0]
        for distance in range(3):
            if distance == 1:
                for copy in stat_copies:
                    copy.wait_recv()


                @pl.when(core == 0)
                def _():
                    for copy in first_copies[2:]:
                        copy.wait_recv()

                for part in (0, 1):
                    far_queries[part].wait_recv()
            stat = stat_out if distance == 0 else stat_in.at[distance - 1]
            query_pos = (seq_at(distance) * rows + iota((rows, columns), 1)).astype(F32)
            turned = (key_pos >= stat[4:5, :]) & (key_pos <= query_pos)
            for h in range(2):
                cols = slice(h * HEAD_DIM, (h + 1) * HEAD_DIM)
                key, value = k_ref[:, cols], v_ref[:, cols]
                if distance == 0:
                    query, grad = q_ref[:, cols], do_ref[:, cols]
                else:
                    query, grad = qd_in[distance - 1, 0, :, cols], qd_in[distance - 1, 1, :, cols]
                score = jnp.where(turned, dot_nt(key, query) * SCALE, OFF)
                prob = jnp.exp(score - stat[h : h + 1, :])
                value_total[h] = value_total[h] + dot(prob.astype(BF16), grad)
                slope = prob * (dot_nt(value, grad) - stat[2 + h : 3 + h, :]) * SCALE
                key_total[h] = key_total[h] + dot(slope.astype(BF16), query)
        for h in range(2):
            cols = slice(h * HEAD_DIM, (h + 1) * HEAD_DIM)
            dk_ref[:, cols] = key_total[h].astype(BF16)
            dv_ref[:, cols] = value_total[h].astype(BF16)


    wait_all(t_dst, n_y - 1, t_recv.at[0])
    wait_all(tl_dst, n_y - 1, tl_recv.at[0])
    carried = jnp.zeros((width, 128), F32)
    for slot in range(n_y):
        grown = jnp.exp(tl_dst[slot]) * carried + t_dst[slot].astype(F32)
        carried = jnp.where(slot < own_group, grown, carried)
    for slot in range(row):
        onward = jnp.where(core == 1, jnp.exp(la_dst[slot]), 1.0)
        r_src[slot] = (onward * (scan_buf[slot] + jnp.exp(cum_buf[slot]) * carried)).astype(BF16)

    def r_copy(other):
        return pltpu.make_async_remote_copy(
            r_src.at[slot_of(other, row, core)],
            state_ref.at[hx, chip, core],
            r_send.at[0],
            r_recv.at[pos],
            (base + other, hx),
            MESH,
        )

    def r_arrival(other):
        return pltpu.make_async_remote_copy(
            r_src.at[0],
            state_ref.at[hx, other // 2, other % 2],
            r_send.at[0],
            r_recv.at[other],
            (base + other, hx),
            MESH,
        )

    def near_first(step):
        return (chip + n_z + (step + 1) // 2 * (2 * (step % 2) - 1)) % n_z

    def x_copy(part, k):
        return pltpu.make_async_remote_copy(
            state_ref.at[hx, part],
            state_ref.at[hx, part],
            state_send.at[k],
            state_recv.at[hx],
            (me, (hx + k) % n_head),
            MESH,
        )

    beside = 2 * chip + 1 - core
    r_copy(beside).start()

    def r_start(step, carry):
        for side in (0, 1):
            r_copy(2 * near_first(step) + side).start()
        return carry

    lax.fori_loop(1, n_z, r_start, 0, unroll=UNROLL)
    state_ref[hx, chip, core] = r_src[own_slot]

    r_arrival(beside).wait_recv()
    for k in head_steps:
        x_copy(chip, k).start()

    def r_pass(step, carry):
        part = near_first(step)
        for side in (0, 1):
            r_arrival(2 * part + side).wait_recv()
        for k in head_steps:
            x_copy(part, k).start()
        return carry

    lax.fori_loop(1, n_z, r_pass, 0, unroll=UNROLL)

    pl.when(core == 0)(lambda: relay(first_copies[:2], pass_keys))
    pl.when(core == 1)(lambda: relay(first_copies[2:], pass_queries))
    forward()
    def entering(head, side):
        return state_ref[head, :, side].reshape(rows, 128)

    y_ref[...] = (
        carry_weight * (y_inner + dot(c_ref[...], entering(hx, 0)))
        + gain_wide * x_ref[...].astype(F32)
    ).astype(BF16)
    xg_ref[...] = (
        source_weight * (x_inner + dot(b_ref[...], entering(hx, 1)))
        + gain_wide * g_ref[...].astype(F32)
    ).astype(BF16)
    inner()
    backward()

    for copy in first_copies + mix_copies + stat_copies:
        copy.wait_send()

    @pl.when(core == 0)
    def _():
        for copy in far_keys + pass_keys:
            copy.wait_send()

    @pl.when(core == 1)
    def _():
        for copy in far_queries + pass_queries:
            copy.wait_send()

    wait_all(a_src, row - 1, a_send.at[0])
    wait_all(la_dst, row - 1, la_send.at[0])
    wait_all(t_dst, n_y - 1, t_send.at[0])
    wait_all(tl_dst, n_y - 1, tl_send.at[0])
    wait_all(r_src, row - 1, r_send.at[0])

    for k in head_steps:
        wait_all(state_ref.at[hx], n_z, state_send.at[k])
    for k in head_steps:
        other = (hx + k) % n_head
        wait_all(state_ref.at[other], n_z, state_recv.at[other])
    bg_ref[...] += sum(dot_nt(mix_ref[h, 1], entering(h, 1)) for h in range(n_head))
    cg_ref[...] += sum(dot_nt(mix_ref[h, 0], entering(h, 0)) for h in range(n_head))


def last_kernel(*refs):
    count = len(refs) // 2
    copies = [
        pltpu.make_async_copy(refs[n], refs[count + n], refs[-1].at[n]) for n in range(count)
    ]
    for copy in copies:
        copy.start()
    for copy in copies:
        copy.wait()


def on_device(
    n_seq,
    n_head,
    n_z,
    queries,
    key_rows,
    value_rows,
    attn_out_grad,
    ssm_input,
    b_matrix,
    c_matrix,
    step_sizes,
    decay_rates,
    skip_gain,
    ssm_out_grad,
    doc_lengths,
):
    rows, columns = queries.shape
    row, n_y, width = 2 * n_z, n_seq // (2 * n_z), rows // n_z
    vmem = pl.BlockSpec(memory_space=pltpu.VMEM)
    hbm = pl.BlockSpec(memory_space=pltpu.HBM)
    states = b_matrix.shape[1]
    shapes = ((rows, columns, BF16),) * 4 + ((rows, 128, BF16),) * 2 + ((rows, states, F32),) * 2
    results = tuple(jax.ShapeDtypeStruct((m, n), kind) for m, n, kind in shapes)
    dma = pltpu.SemaphoreType.DMA
    outs = pl.pallas_call(
        functools.partial(main_kernel, n_seq, n_head, n_z),
        out_shape=results,
        in_specs=[hbm] * 12,
        out_specs=(vmem,) * 8,
        scratch_shapes=[
            pltpu.VMEM((n_head, 2, rows, 128), BF16),
            pltpu.VMEM((n_head, n_z, 2, width, 128), BF16),
            pltpu.VMEM((rows, columns), BF16),
            pltpu.VMEM((rows, columns), BF16),
            pltpu.VMEM((rows, columns), BF16),
            pltpu.VMEM((rows, columns), BF16),
            pltpu.VMEM((rows, 128), BF16),
            pltpu.VMEM((rows, 128), BF16),
            pltpu.VMEM((rows, states), BF16),
            pltpu.VMEM((rows, states), BF16),
            pltpu.SMEM(decay_rates.shape, F32),
            pltpu.SMEM(skip_gain.shape, F32),
            pltpu.VMEM((1, doc_lengths.shape[0]), jnp.int32),
            pltpu.VMEM((step_sizes.shape[1], rows), F32),
            dma((12,)),
            pltpu.VMEM((2, 2, rows, columns), BF16),
            pltpu.VMEM((2, 2, rows, columns), BF16),
            pltpu.VMEM((8, rows), F32),
            pltpu.VMEM((2, 8, rows), F32),
            pltpu.VMEM((row, width, 128), BF16),
            pltpu.VMEM((row, width, 128), BF16),
            pltpu.VMEM((1, 128), F32),
            pltpu.VMEM((row, 1, 128), F32),
            pltpu.VMEM((row, width, 128), F32),
            pltpu.VMEM((row, 1, 128), F32),
            pltpu.VMEM((width, 128), BF16),
            pltpu.VMEM((n_y, width, 128), BF16),
            pltpu.VMEM((1, 128), F32),
            pltpu.VMEM((n_y, 1, 128), F32),
            pltpu.VMEM((row, width, 128), BF16),
            dma((8,)),
            dma((8,)),
            dma((2,)),
            dma((2,)),
            *[dma((1,))] * 9,
            dma((row,)),
            dma((n_head,)),
            dma((n_head,)),
            dma((n_head,)),
            dma((n_head,)),
        ],
        compiler_params=pltpu.CompilerParams(
            collective_id=0, has_side_effects=True, vmem_limit_bytes=VMEM_BYTES
        ),
        name="main",
    )(
        *[
            pltpu.with_memory_space_constraint(array, pltpu.HBM)
            for array in (
                decay_rates,
                skip_gain,
                doc_lengths.reshape(1, -1),
                step_sizes.T,
                queries,
                key_rows,
                value_rows,
                attn_out_grad,
                ssm_input,
                ssm_out_grad,
                b_matrix,
                c_matrix,
            )
        ],
    )
    return pl.pallas_call(
        last_kernel,
        out_shape=results,
        in_specs=[vmem] * 8,
        out_specs=(hbm,) * 8,
        scratch_shapes=[dma((8,))],
        compiler_params=pltpu.CompilerParams(vmem_limit_bytes=VMEM_BYTES),
        name="last",
    )(*outs)


def build(mesh, n_z):
    n_seq, n_head = mesh.shape["seq"], mesh.shape["head"]
    tokens = P("seq", "head")
    whole = P("seq", None)
    return jax.shard_map(
        functools.partial(on_device, n_seq, n_head, n_z),
        mesh=mesh,
        in_specs=(
            tokens,
            tokens,
            tokens,
            tokens,
            tokens,
            whole,
            whole,
            tokens,
            P("head"),
            P("head"),
            tokens,
            P(),
        ),
        out_specs=(tokens, tokens, tokens, tokens, tokens, tokens, whole, whole),
        check_vma=False,
    )


def solution(mesh):
    return build(mesh, 8)
```
